256 devices in a mesh: dp: 64 (over x, y_lo, z), fsdp: 4 (over y_hi, core).
Axes of the slice: x: 4, y: 4 (y_hi: 2, y_lo: 2; y = y_hi * 2 + y_lo), z: 8, core: 2. Of those that a mesh axis runs over, the one named last changes fastest.
Arguments:
- frames: bfloat16 [64, 4, 48, 64, 128], P('dp', 'fsdp'), may hold values from -6 to 6
- occupied_slot_counts: int32 [4, 64], P('fsdp', 'dp'), may hold values from 1 to 48, 1024 in all within a row
- block_frame_rows: int32 [64, 4, 48], P('dp', 'fsdp'), may hold values from 1 to 16
- order: int32 [4, 64], P('fsdp'), may hold values from 0 to 63, each once within a row
- cotangent: bfloat16 [64, 4, 16, 16, 1536], P('dp', 'fsdp'), may hold values from -6 to 6
- sub_weight: bfloat16 [512, 1536], P('fsdp'), may hold values from -0.25 to 0.25
- depth_kernel: float32 [31, 1536], replicated, may hold values from -1 to 1
- norm_gain: float32 [1536], replicated, may hold values from 0.5 to 1.5
- w_in: bfloat16 [1536, 3072], P('fsdp'), may hold values from -0.15625 to 0.15625
- w_out: bfloat16 [3072, 1536], P('fsdp'), may hold values from -0.109375 to 0.109375
Outputs:
- grad_in: bfloat16 [64, 1536, 3072], P('dp', 'fsdp')
- grad_out: bfloat16 [64, 3072, 1536], P('dp', 'fsdp')
- kernel_grad: float32 [31, 1536], replicated
The draws below stay inside these ranges and needn't reach their ends.
Inputs may be any that keep to these rules, and one draw needn't show every extreme that they name: `occupied_slot_counts`: for each fsdp index the 64 counts sum to 1024, and the largest is 48.
All inputs are finite; a program needn't handle non-finite values. No bound on the sum of `occupied_slot_counts` on one device may be relied on, other than what follows from the above.
Results may differ from the reference program's by a relative error of at most 0.02.
Values may be sent and summed in bfloat16 or wider, within the bound.
A program may use at most 128 MiB of HBM per device.

```python
import math
import jax
import jax.numpy as jnp
import numpy as np
from jax import lax

D = 1536
FF = 3072
MEL = 128
K = 31
BR = 16
BIN = 64
NB = 16
NH = 48
N_DP = 64
N_FSDP = 4


def with_ends(drawn, own_key, smallest, largest):
    longest = drawn.shape.index(max(drawn.shape))
    spots = []
    for shift in (0, 1):
        where = [jax.random.randint(jax.random.fold_in(own_key, axis), (), 0, length) for axis, length in enumerate(drawn.shape)]
        where[longest] = (where[longest] + shift) % drawn.shape[longest]
        spots.append(tuple(where))
    return drawn.at[spots[0]].set(smallest).at[spots[1]].set(largest)


def block_scale(stream_key, shape, cuts, smallest, largest):
    factor_of = 1.0
    for dim, blocks in cuts:
        heights = jax.random.uniform(jax.random.fold_in(jax.random.fold_in(stream_key, 6), dim), (blocks,), jnp.float32, smallest / len(cuts), largest / len(cuts))
        factor_of = factor_of * jnp.repeat(jnp.exp(heights), shape[dim] // blocks).reshape((-1,) + (1,) * (len(shape) - 1 - dim))
    return factor_of


def split_up(count, total, bound, lean):
    weights = [(1 << 20) // math.isqrt(rank ** lean) + 1 for rank in range(2, count + 1)]
    surplus, given = total - bound - (count - 1), [1] * (count - 1)
    while surplus > 0:
        free = [i for i in range(count - 1) if given[i] < bound]
        mass, remaining = sum([weights[i] for i in free]), surplus
        for i in free:
            addition = min(bound - given[i], max(1, remaining * weights[i] // mass), surplus)
            given[i] = given[i] + addition
            surplus = surplus - addition
    return np.array([bound] + given)


def ragged(rng, amount, total, limit, lean):
    if amount == 2:
        one = jax.random.randint(rng, (), max(1, total - limit), min(limit, total - 1) + 1)
        return jnp.stack([one, total - one])
    sizes = jnp.asarray(split_up(amount, total, limit, lean), jnp.int32)
    pairs = (amount - 1) // 2
    giver, taker = sizes[1:1 + 2 * pairs:2], sizes[2:2 + 2 * pairs:2]
    margin = jnp.minimum(giver - 1, limit - taker)
    shifted = jax.random.randint(jax.random.fold_in(rng, 1), (pairs,), 0, 1 << 20) % (margin + 1)
    sizes = sizes.at[1:1 + 2 * pairs:2].set(giver - shifted).at[2:2 + 2 * pairs:2].set(taker + shifted)
    return sizes[jax.random.permutation(jax.random.fold_in(rng, 2), amount)]


def scatter_about(rng, dims, scale, limit, pieces=(), held_as=jnp.bfloat16):
    factor_of = block_scale(rng, dims, pieces, -0.22, 0.18) if pieces else 1.0
    drawn = jax.random.normal(rng, dims, jnp.float32) * scale * factor_of
    return jnp.minimum(jnp.maximum(drawn, -limit), limit).astype(held_as)


def setup_inputs(seed: int = 0) -> dict:
    splits = jax.random.split(jax.random.key(seed), 11)
    return {
        "frames": scatter_about(splits[0], (N_DP, N_FSDP, NH, BIN, MEL), 1.0, 6.0, ((0, 64), (1, 4))),
        "occupied_slot_counts": jax.vmap(lambda own: ragged(own, N_DP, N_DP * NB, NH, 2))(jax.random.split(splits[1], N_FSDP)).reshape((N_FSDP, N_DP)).astype(jnp.int32),
        "block_frame_rows": with_ends(jax.random.randint(splits[2], (N_DP, N_FSDP, NH), 1, BR + 1), jax.random.fold_in(splits[2], 1), 1, BR).astype(jnp.int32),
        "order": jax.vmap(lambda own: jax.random.permutation(own, N_DP))(jax.random.split(splits[3], N_FSDP)).reshape((N_FSDP, N_DP)).astype(jnp.int32),
        "cotangent": scatter_about(splits[4], (N_DP, N_FSDP, NB, BR, D), 1.0, 6.0, ((0, 64), (1, 4))),
        "sub_weight": scatter_about(splits[5], (4 * MEL, D), (4 * MEL) ** -0.5, 0.25, ((0, 4),)),
        "depth_kernel": scatter_about(splits[6], (K, D), K ** -0.5, 1.0, (), jnp.float32),
        "norm_gain": jnp.clip(1.0 + 0.1 * jax.random.normal(splits[7], (D,), jnp.float32), 0.5, 1.5),
        "w_in": scatter_about(splits[8], (D, FF), D ** -0.5, 0.15625, ((0, 4),)),
        "w_out": scatter_about(splits[9], (FF, D), FF ** -0.5, 0.109375, ((0, 4),)),
    }


EPSILON = 1e-05

def swish_slope(values):
    sigma = jax.nn.sigmoid(values)
    return sigma * (1.0 + values * (1.0 - sigma))

def layer_norm(mixed, norm_gain):
    mean_value = lax.optimization_barrier(jnp.mean(mixed, axis=-1, keepdims=True))
    centred = mixed - mean_value
    variance = lax.optimization_barrier(jnp.mean(centred * centred, axis=-1, keepdims=True))
    return centred * lax.rsqrt(variance + EPSILON) * norm_gain

def padded_blocks(features, tap_count):
    half_span = (tap_count - 1) // 2
    return jnp.pad(features, ((0, 0), (half_span, half_span), (0, 0)))

def depthwise(features, depth_kernel):
    tap_count = depth_kernel.shape[0]
    steps_len = features.shape[1]
    padded = padded_blocks(features, tap_count)
    running = jnp.zeros(features.shape, features.dtype)
    for tap_index in range(tap_count):
        running = running + padded[:, tap_index:tap_index + steps_len, :] * depth_kernel[tap_index]
    return running

def kernel_terms(conv_grad, features, tap_count):
    steps_len = features.shape[1]
    padded = padded_blocks(features, tap_count)
    columns = [lax.optimization_barrier(jnp.sum(conv_grad * padded[:, tap_index:tap_index + steps_len, :], axis=(0, 1))) for tap_index in range(tap_count)]
    return jnp.stack(columns)

def contract(left, right, left_dim, right_dim):
    return lax.dot_general(left, right, (((left_dim,), (right_dim,)), ((), ())), preferred_element_type=jnp.float32)

def balanced_blocks(frames, occupied_slot_counts, block_frame_rows, order, data_parallel_index, sharded_parallel_index):
    counts = occupied_slot_counts[sharded_parallel_index]
    ends = jnp.cumsum(counts, dtype=jnp.int32)
    starts = ends - counts
    slot_index = jnp.arange(N_DP, dtype=jnp.int32)
    first = jnp.sum(jnp.where(order[sharded_parallel_index] == data_parallel_index, slot_index, 0), dtype=jnp.int32)
    global_index = first + jnp.arange(NB, dtype=jnp.int32) * N_DP
    source = lax.optimization_barrier(jnp.sum((ends[None, :] <= global_index[:, None]).astype(jnp.int32), axis=1, dtype=jnp.int32))
    within = global_index - starts[source]
    return (frames[source, sharded_parallel_index, within], block_frame_rows[source, sharded_parallel_index, within])

def device_step(frame_blocks, valid_row_counts, cot_blocks, sub_weight, depth_kernel, norm_gain, w_in, w_out):
    block_total = frame_blocks.shape[0]
    row_total = block_total * BR
    row_mask = (jnp.arange(BR, dtype=jnp.int32)[None, :] < valid_row_counts[:, None]).astype(jnp.float32).reshape(row_total, 1)
    patches = frame_blocks.reshape(row_total, 4 * MEL)
    features = (jnp.dot(patches, sub_weight, preferred_element_type=jnp.float32) * row_mask).astype(jnp.bfloat16)
    feature_blocks = lax.optimization_barrier(features).astype(jnp.float32).reshape(block_total, BR, D)
    block_mask = row_mask.reshape(block_total, BR, 1)
    conv_out = depthwise(feature_blocks, depth_kernel)
    mixed = feature_blocks + block_mask * conv_out * jax.nn.sigmoid(conv_out)
    mixed_rows = mixed.reshape(row_total, D)
    normed = layer_norm(mixed_rows, norm_gain).astype(jnp.bfloat16)
    pre_act = jnp.dot(normed, w_in, preferred_element_type=jnp.float32)
    hidden = (pre_act * jax.nn.sigmoid(pre_act)).astype(jnp.bfloat16)
    masked_cot = jnp.where(row_mask > 0, cot_blocks.reshape(row_total, D), jnp.zeros((), cot_blocks.dtype))
    hidden_grad = 0.5 * contract(masked_cot, w_out, 1, 1)
    pre_grad = (hidden_grad * swish_slope(pre_act)).astype(jnp.bfloat16)
    term_in = contract(normed, pre_grad, 0, 0)
    term_out = 0.5 * contract(hidden, masked_cot, 0, 0)
    normed_grad = contract(pre_grad, w_in, 1, 1)
    norm_pullback = jax.vjp(lambda values: layer_norm(values, norm_gain), mixed_rows)[1]
    mixed_grad = masked_cot.astype(jnp.float32) + norm_pullback(normed_grad)[0]
    conv_grad = block_mask * mixed_grad.reshape(block_total, BR, D) * swish_slope(conv_out)
    kernel_part = kernel_terms(conv_grad, feature_blocks, depth_kernel.shape[0])
    return (term_in, term_out, kernel_part)

def reference(frames, occupied_slot_counts, block_frame_rows, order, cotangent, sub_weight, depth_kernel, norm_gain, w_in, w_out):

    def one_group(data_parallel_index):
        grad_in_total = jnp.zeros((D, FF), jnp.float32)
        grad_out_total = jnp.zeros((FF, D), jnp.float32)
        kernel_total = jnp.zeros(depth_kernel.shape, jnp.float32)
        group_cot = lax.dynamic_index_in_dim(cotangent, data_parallel_index, 0, keepdims=False)
        for sharded_parallel_index in range(N_FSDP):
            frame_blocks, valid_row_counts = balanced_blocks(frames, occupied_slot_counts, block_frame_rows, order, data_parallel_index, sharded_parallel_index)
            term_in, term_out, kernel_part = device_step(frame_blocks, valid_row_counts, group_cot[sharded_parallel_index], sub_weight, depth_kernel, norm_gain, w_in, w_out)
            grad_in_total = grad_in_total + lax.optimization_barrier(term_in.astype(jnp.bfloat16)).astype(jnp.float32)
            grad_out_total = grad_out_total + lax.optimization_barrier(term_out.astype(jnp.bfloat16)).astype(jnp.float32)
            kernel_total = kernel_total + kernel_part
        return (grad_in_total.astype(jnp.bfloat16), grad_out_total.astype(jnp.bfloat16), kernel_total)
    grad_in, grad_out, kernel_parts = lax.map(one_group, jnp.arange(N_DP, dtype=jnp.int32))
    kernel_grad = lax.optimization_barrier(jnp.sum(kernel_parts, axis=0)) / (NB * BR)
    return (grad_in, grad_out, kernel_grad)
```

```python
import functools

import jax
import jax.numpy as jnp
from jax import lax
from jax.experimental import pallas as pl
from jax.experimental.pallas import tpu as pltpu
from jax.sharding import PartitionSpec as P

D = 1536
FF = 3072
K = 31
BR = 16
NB = 16
NH = 48
NDP = 64
ROWS = NB * BR
HALF = FF // 2
FSH = FF // 4
DSH = D // 4
SSH = 128
EPSILON = 1e-05
MESH = pl.DeviceIdType.MESH
F32 = jnp.float32
BF16 = jnp.bfloat16
VLIM = 60 * 1024 * 1024

ANY = pl.BlockSpec(memory_space=pl.ANY)
VM = pl.BlockSpec(memory_space=pltpu.VMEM)
SM = pl.BlockSpec(memory_space=pltpu.SMEM)


def place():
    dp, f = lax.axis_index("dp"), lax.axis_index("fsdp")
    return dp, f, dp // 16, (dp // 8) % 2, dp % 8, f // 2, f % 2


def dev(x, yl, z, yh, c):
    return ((x * 2 + yl) * 8 + z, yh * 2 + c)


def greet(peers, extra=0):
    bar = pltpu.get_barrier_semaphore()
    for peer in peers:
        pl.semaphore_signal(bar, inc=1, device_id=peer, device_id_type=MESH)
    pl.semaphore_wait(bar, len(peers) + extra)


def remote(src, dst, send, recv, device):
    return pltpu.make_async_remote_copy(
        src_ref=src, dst_ref=dst, send_sem=send, recv_sem=recv, device_id=device, device_id_type=MESH
    )


class Sent:
    def __init__(self, src, dst, ss, rs, i, device):
        self.sems, self.device = (ss.at[i], rs.at[i]), device
        self.copy = remote(src, dst, *self.sems, device)

    def start(self):
        self.copy.start()

    def wait(self):
        self.copy.wait()

    def wait_send(self):
        self.copy.wait_send()

    def wait_got(self, ref):
        remote(ref, ref, *self.sems, self.device).wait_recv()


def meta_kernel(mine, table, ss, rs, gs, gr):
    dp, f, x, yl, z, yh, c = place()
    mates = [(dp, yh * 2 + 1 - c), (dp, (1 - yh) * 2 + c), (dp, (1 - yh) * 2 + 1 - c)]
    bar = pltpu.get_barrier_semaphore()

    def signal(k, carry):
        pl.semaphore_signal(bar, inc=1, device_id=(lax.rem(dp + k, NDP), f), device_id_type=MESH)
        return carry

    lax.fori_loop(1, NDP, signal, 0)
    greet(mates, NDP - 1)
    table[pl.ds(f * NDP, 1)] = mine[...]

    def send(k, carry):
        to = lax.rem(dp + k, NDP)
        row = pl.ds(f * NDP + k, 1)
        remote(mine, table.at[row], ss, rs, (to, f)).start()
        return carry

    lax.fori_loop(1, NDP, send, 0)
    rest = table.at[pl.ds(f * NDP + 1, NDP - 1)]
    remote(rest, rest, ss, rs, mates[0]).wait()
    whole = table.at[pl.ds(f * NDP, NDP)]
    copies = [remote(whole, whole, gs.at[i], gr.at[i], mate) for i, mate in enumerate(mates)]
    for copy in copies:
        copy.start()
    for copy in copies:
        copy.wait()


def group_table(mine):
    return pl.pallas_call(
        meta_kernel,
        out_shape=jax.ShapeDtypeStruct((4 * NDP, 1, 128), jnp.int32),
        in_specs=[VM],
        out_specs=VM,
        scratch_shapes=[
            pltpu.SemaphoreType.DMA,
            pltpu.SemaphoreType.DMA,
            pltpu.SemaphoreType.DMA((3,)),
            pltpu.SemaphoreType.DMA((3,)),
        ],
        compiler_params=pltpu.CompilerParams(collective_id=1, has_side_effects=True),
        name="group_table",
    )(mine)


def move_kernel(
    hsel, slot, frames, cot, w_in, w_out, sub,
    blocks, cots, winh, wouth, suba, stage,
    sbuf, rbuf, as_, ar, ss, rs, ls,
):
    dp, f, x, yl, z, yh, c = place()
    fo, fs, fso = (1 - yh) * 2 + c, yh * 2 + 1 - c, (1 - yh) * 2 + 1 - c
    color = lax.rem(x + 2 * z, 4)
    across = dev(x, 1 - yl, z, 1 - yh, c)
    other = (dp, fo)
    sibling = (dp, fs)
    xp, xm = dev(lax.rem(x + 1, 4), yl, z, yh, c), dev(lax.rem(x + 3, 4), yl, z, yh, c)
    zp, zm = dev(x, yl, lax.rem(z + 1, 8), yh, c), dev(x, yl, lax.rem(z + 7, 8), yh, c)
    bar = pltpu.get_barrier_semaphore()

    def signal(k, carry):
        pl.semaphore_signal(bar, inc=1, device_id=(lax.rem(dp + k, NDP), f), device_id_type=MESH)
        return carry

    lax.fori_loop(1, NDP, signal, 0)
    greet([across, other, sibling], NDP - 1)

    count = iter(range(64))

    def rcopy(src, dst, device):
        return Sent(src, dst, ss, rs, next(count), device)

    def cols(g):
        return pl.ds(pl.multiple_of(g * FSH, FSH), FSH)

    def rows(start, size):
        return pl.ds(pl.multiple_of(start, 16), size)

    lo, hi = pl.ds(0, FSH), pl.ds(FSH, FSH)
    q = rows(color * (DSH // 4), DSH // 4)
    qd = rows(f * DSH + color * (DSH // 4), DSH // 4)
    y_sub = [rcopy(sub.at[rows(color * 32, 32)], suba.at[rows(f * SSH + color * 32, 32)], across)]
    y_out = [rcopy(w_out.at[rows(color * 192, 192)], wouth.at[rows(FSH + color * 192, 192)], across)]
    y_in = [
        rcopy(w_in.at[q, cols(fo)], winh.at[qd, lo], across),
        rcopy(w_in.at[q, cols(f)], winh.at[qd, hi], across),
        rcopy(w_in.at[q, cols(fso)], stage.at[q, lo], across),
        rcopy(w_in.at[q, cols(fs)], stage.at[q, hi], across),
    ]
    for copy in y_sub + y_out + y_in:
        copy.start()
    cot_other = rcopy(cot, cots.at[1], other)
    cot_other.start()
    mine = rows(f * DSH, DSH)
    on_chip = [
        rcopy(sub, suba.at[rows(f * SSH, SSH)], sibling),
        rcopy(cot, cots.at[2], sibling),
        rcopy(w_in.at[:, cols(fs)], winh.at[mine, lo], sibling),
        rcopy(w_in.at[:, cols(fso)], winh.at[mine, hi], sibling),
    ]
    local = [
        pltpu.make_async_copy(cot, cots.at[0], ls.at[0]),
        pltpu.make_async_copy(sub, suba.at[rows(f * SSH, SSH)], ls.at[1]),
        pltpu.make_async_copy(w_out, wouth.at[pl.ds(0, FSH)], ls.at[2]),
        pltpu.make_async_copy(w_in.at[:, cols(f)], winh.at[mine, lo], ls.at[3]),
        pltpu.make_async_copy(w_in.at[:, cols(fo)], winh.at[mine, hi], ls.at[4]),
    ]
    for copy in on_chip + local:
        copy.start()

    def pack(j, carry):
        sbuf[j] = frames[hsel[j]]
        return carry

    lax.fori_loop(0, NDP, pack, 0)

    def send(k, carry):
        to = lax.rem(dp + k, NDP)
        remote(sbuf.at[to], rbuf.at[k], as_, ar, (to, f)).start()
        return carry

    lax.fori_loop(1, NDP, send, 0)
    rbuf[0] = sbuf[dp]

    def forward(ref, start, size):
        a = start + color * size
        full, first, second = rows(a, size), rows(a, size // 2), rows(a + size // 2, size // 2)
        copies = [
            rcopy(ref.at[full], ref.at[full], xp),
            rcopy(ref.at[full], ref.at[full], xm),
            rcopy(ref.at[first], ref.at[first], zp),
            rcopy(ref.at[second], ref.at[second], zm),
        ]
        for copy in copies:
            copy.start()
        left, right = start + lax.rem(color + 3, 4) * size, start + lax.rem(color + 1, 4) * size
        far = start + lax.rem(color + 2, 4) * size
        spots = [rows(left, size), rows(right, size), rows(far, size // 2), rows(far + size // 2, size // 2)]
        return [(copy, ref.at[spot]) for copy, spot in zip(copies, spots)]

    y_sub[0].wait_send()
    y_sub[0].wait_got(suba.at[rows(fo * SSH + color * 32, 32)])
    arrive_sub = forward(suba, fo * SSH, 32)
    y_out[0].wait()
    arrive_out = forward(wouth, FSH, 192)
    for copy in y_in:
        copy.wait_send()
    qi = rows(fo * DSH + color * (DSH // 4), DSH // 4)
    for copy, ref in zip(y_in, [winh.at[qi, lo], winh.at[qi, hi], stage.at[q, lo], stage.at[q, hi]]):
        copy.wait_got(ref)
    arrive_in = forward(winh, fo * DSH, DSH // 4)
    arrive_stage = forward(stage, 0, DSH // 4)

    every = rbuf.at[pl.ds(1, NDP - 1)]
    remote(every, every, as_, ar, other).wait()

    def select(m, carry):
        blocks[m] = rbuf[slot[m]]
        return carry

    lax.fori_loop(0, NB, select, 0)
    fwd_blocks = rcopy(blocks.at[pl.ds(0, NB)], blocks.at[pl.ds(NB, NB)], other)
    fwd_blocks.start()

    def settle(pairs):
        for copy, ref in pairs:
            copy.wait_send()
        for copy, ref in pairs:
            copy.wait_got(ref)

    settle(arrive_sub)
    theirs = suba.at[rows(fo * SSH, SSH)]
    sub_sib = rcopy(theirs, theirs, sibling)
    sub_sib.start()
    cot_other.wait()
    cot_sib = rcopy(cots.at[1], cots.at[3], sibling)
    cot_sib.start()
    settle(arrive_out)
    settle(arrive_in)
    settle(arrive_stage)
    stage_sib = rcopy(stage, winh.at[rows(fo * DSH, DSH)], sibling)
    stage_sib.start()
    for copy in on_chip:
        copy.wait_send()
    for ref, copy in zip(
        [suba.at[rows(fs * SSH, SSH)], cots.at[2], winh.at[rows(fs * DSH, DSH), lo], winh.at[rows(fs * DSH, DSH), hi]],
        on_chip,
    ):
        copy.wait_got(ref)
    for copy in local:
        copy.wait()
    fwd_blocks.wait()
    sub_sib.wait_send()
    sub_sib.wait_got(suba.at[rows(fso * SSH, SSH)])
    cot_sib.wait()
    stage_sib.wait_send()
    stage_sib.wait_got(winh.at[rows(fso * DSH, DSH)])


def move(hsel, slot, frames, cot, w_in, w_out, sub):
    return pl.pallas_call(
        move_kernel,
        out_shape=[
            jax.ShapeDtypeStruct((2 * NB, 64, 128), BF16),
            jax.ShapeDtypeStruct((4, ROWS, D), BF16),
            jax.ShapeDtypeStruct((D, HALF), BF16),
            jax.ShapeDtypeStruct((HALF, D), BF16),
            jax.ShapeDtypeStruct((4 * SSH, D), BF16),
            jax.ShapeDtypeStruct((DSH, HALF), BF16),
        ],
        in_specs=[SM, SM, VM, ANY, ANY, ANY, ANY],
        out_specs=[VM, ANY, ANY, ANY, ANY, ANY],
        scratch_shapes=[
            pltpu.VMEM((NDP, 64, 128), BF16),
            pltpu.VMEM((NDP, 64, 128), BF16),
            pltpu.SemaphoreType.DMA,
            pltpu.SemaphoreType.DMA,
            pltpu.SemaphoreType.DMA((32,)),
            pltpu.SemaphoreType.DMA((32,)),
            pltpu.SemaphoreType.DMA((5,)),
        ],
        compiler_params=pltpu.CompilerParams(collective_id=2, has_side_effects=True),
        name="move",
    )(hsel, slot, frames, cot, w_in, w_out, sub)


def front_kernel(blocks, suba, cots, masks, taps, gain, masked, feat, conv, normed, ftmp):
    r = lax.broadcasted_iota(jnp.int32, (ROWS, ROWS), 0)
    col = lax.broadcasted_iota(jnp.int32, (ROWS, ROWS), 1)
    turn = jnp.where(col == lax.rem(r, NB) * BR + r // NB, 1.0, 0.0).astype(BF16)
    for g in range(4):
        mask = masks[g] > 0
        moved = jnp.dot(turn, cots[g], preferred_element_type=F32)
        masked[g] = jnp.where(mask, moved, 0.0).astype(BF16)
    r = lax.broadcasted_iota(jnp.int32, (ROWS, 4 * ROWS), 0)
    col = lax.broadcasted_iota(jnp.int32, (ROWS, 4 * ROWS), 1)
    want = lax.rem(r, NB) * (4 * BR) + 4 * (r // NB)
    for g in range(2):
        mask = masks[g]
        frames = blocks[pl.ds(g * NB, NB)].reshape(4 * ROWS, 128)
        total = jnp.zeros((ROWS, D), F32)
        for k in range(4):
            pick = jnp.where(col == want + k, 1.0, 0.0).astype(BF16)
            patch = jnp.dot(pick, frames, preferred_element_type=F32).astype(BF16)
            total += jnp.dot(patch, suba[pl.ds(k * 128, 128)], preferred_element_type=F32)
        feat[g] = (total * mask).astype(BF16)

        def chunk(l, carry):
            lanes = pl.ds(pl.multiple_of(l * 128, 128), 128)
            rows = [feat[g, pl.ds(t * NB, NB), lanes].astype(F32) for t in range(BR)]
            for t in range(BR):
                acc = None
                for s in range(BR):
                    tap = taps[pl.ds(s - t + 15, 1), lanes]
                    term = rows[s] * tap
                    acc = term if acc is None else acc + term
                if g == 0:
                    conv[pl.ds(t * NB, NB), lanes] = acc
                ftmp[pl.ds(t * NB, NB), lanes] = rows[t] + masks[g, pl.ds(t * NB, NB)] * (acc * jax.nn.sigmoid(acc))
            return carry

        lax.fori_loop(0, D // 128, chunk, 0)
        mixed = ftmp[...]
        mean = jnp.mean(mixed, axis=-1, keepdims=True)
        centred = mixed - mean
        variance = jnp.mean(centred * centred, axis=-1, keepdims=True)
        normed[g] = (centred * lax.rsqrt(variance + EPSILON) * gain[...]).astype(BF16)


def front(blocks, suba, cots, masks, taps, gain):
    return pl.pallas_call(
        front_kernel,
        out_shape=[
            jax.ShapeDtypeStruct((4, ROWS, D), BF16),
            jax.ShapeDtypeStruct((2, ROWS, D), BF16),
            jax.ShapeDtypeStruct((ROWS, D), F32),
            jax.ShapeDtypeStruct((2, ROWS, D), BF16),
        ],
        in_specs=[VM] * 6,
        out_specs=[VM] * 4,
        scratch_shapes=[pltpu.VMEM((ROWS, D), F32)],
        compiler_params=pltpu.CompilerParams(vmem_limit_bytes=VLIM),
        name="front",
    )(blocks, suba, cots, masks, taps, gain)


def nt(left, right):
    return lax.dot_general(left, right, (((1,), (1,)), ((), ())), preferred_element_type=F32)


def tn(left, right):
    return lax.dot_general(left, right, (((0,), (0,)), ((), ())), preferred_element_type=F32)


def middle_kernel(normed, masked, winh, wouth, nall, pgrad, hidden, ngrad, part, got, ss, rs):
    dp, f, x, yl, z, yh, c = place()
    sibling = (dp, yh * 2 + 1 - c)
    greet([sibling])
    swaps = [remote(normed.at[g], nall.at[2 + g], ss.at[g], rs.at[g], sibling) for g in range(2)]
    for swap in swaps:
        swap.start()
    nall[0] = normed[0]
    nall[1] = normed[1]

    def group(g):
        def tile(n, carry):
            w = pl.ds(pl.multiple_of(n * 256, 256), 256)
            pre = jnp.dot(nall[g], winh[:, w], preferred_element_type=F32)
            hgrad = 0.5 * nt(masked[g], wouth[w, :])
            sig = jax.nn.sigmoid(pre)
            hidden[g, :, w] = (pre * sig).astype(BF16)
            pgrad[g, :, w] = (hgrad * (sig * (1.0 + pre * (1.0 - sig)))).astype(BF16)
            return carry

        lax.fori_loop(0, HALF // 256, tile, 0)

    def back(g, ref):
        def tile(n, carry):
            w = pl.ds(pl.multiple_of(n * 256, 256), 256)
            ref[:, w] = nt(pgrad[g], winh[w, :])
            return carry

        lax.fori_loop(0, D // 256, tile, 0)

    group(0)
    swaps[0].wait()
    group(2)
    back(2, part)
    give = remote(part, got, ss.at[2], rs.at[2], sibling)
    give.start()
    back(0, ngrad)
    group(1)
    swaps[1].wait()
    group(3)
    give.wait()
    ngrad[...] += got[...]


def middle(normed, masked, winh, wouth):
    return pl.pallas_call(
        middle_kernel,
        out_shape=[
            jax.ShapeDtypeStruct((4, ROWS, D), BF16),
            jax.ShapeDtypeStruct((4, ROWS, HALF), BF16),
            jax.ShapeDtypeStruct((4, ROWS, HALF), BF16),
            jax.ShapeDtypeStruct((ROWS, D), F32),
        ],
        in_specs=[VM] * 4,
        out_specs=[VM] * 4,
        scratch_shapes=[
            pltpu.VMEM((ROWS, D), F32),
            pltpu.VMEM((ROWS, D), F32),
            pltpu.SemaphoreType.DMA((3,)),
            pltpu.SemaphoreType.DMA((3,)),
        ],
        compiler_params=pltpu.CompilerParams(collective_id=3, has_side_effects=True, vmem_limit_bytes=VLIM),
        name="middle",
    )(normed, masked, winh, wouth)


def taps_kernel(ngrad, masked, feat, conv, masks, gain, out, dmix):
    mask = masks[0]
    pre = conv[...]
    mixed = feat[0].astype(F32) + mask * (pre * jax.nn.sigmoid(pre))
    mean = jnp.mean(mixed, axis=-1, keepdims=True)
    centred = mixed - mean
    scale = lax.rsqrt(jnp.mean(centred * centred, axis=-1, keepdims=True) + EPSILON)
    hat = centred * scale
    dn = ngrad[...] * gain[...]
    m1 = jnp.mean(dn, axis=-1, keepdims=True)
    m2 = jnp.mean(dn * hat, axis=-1, keepdims=True)
    total = masked[0].astype(F32) + scale * (dn - m1 - hat * m2)
    sig = jax.nn.sigmoid(pre)
    dmix[...] = mask * total * (sig * (1.0 + pre * (1.0 - sig)))

    def chunk(l, carry):
        lanes = pl.ds(pl.multiple_of(l * 128, 128), 128)
        frows = [feat[0, pl.ds(s * NB, NB), lanes].astype(F32) for s in range(BR)]
        sums = [None] * K
        for t in range(BR):
            g = dmix[pl.ds(t * NB, NB), lanes]
            for s in range(BR):
                term = g * frows[s]
                k = s - t + 15
                sums[k] = term if sums[k] is None else sums[k] + term
        for k in range(K):
            out[l, pl.ds(k, 1), :] = jnp.sum(sums[k], axis=0, keepdims=True)
        out[l, pl.ds(K, 1), :] = jnp.zeros((1, 128), F32)
        return carry

    lax.fori_loop(0, D // 128, chunk, 0)


def tap_terms(ngrad, masked, feat, conv, masks, gain):
    return pl.pallas_call(
        taps_kernel,
        out_shape=jax.ShapeDtypeStruct((D // 128, K + 1, 128), F32),
        in_specs=[VM] * 6,
        out_specs=VM,
        scratch_shapes=[pltpu.VMEM((ROWS, D), F32)],
        compiler_params=pltpu.CompilerParams(vmem_limit_bytes=VLIM),
        name="tap_terms",
    )(ngrad, masked, feat, conv, masks, gain)


def last_kernel(part, nall, pgrad, hidden, masked, gin, gout, ktot, r1, s1, r2, s2, r3, give, ss, rs, gs, gr):
    dp, f, x, yl, z, yh, c = place()
    y = yh * 2 + yl
    near, far = z * 2 + c, x * 4 + y
    fo, fs = (1 - yh) * 2 + c, yh * 2 + 1 - c

    def near_dev(i):
        return dev(x, yl, i // 2, yh, lax.rem(i, 2))

    def far_dev(i):
        return dev(i // 4, lax.rem(i, 2), z, lax.rem(i, 4) // 2, c)

    bar = pltpu.get_barrier_semaphore()

    def signal(k, carry):
        pl.semaphore_signal(bar, inc=1, device_id=near_dev(lax.rem(near + k, 16)), device_id_type=MESH)
        pl.semaphore_signal(bar, inc=1, device_id=far_dev(lax.rem(far + k, 16)), device_id_type=MESH)
        return carry

    lax.fori_loop(1, 16, signal, 0)
    pl.semaphore_wait(bar, 30)

    def spread(make, stage):
        def step(k, carry):
            make(k).start()
            return carry

        lax.fori_loop(1, 16, step, 0)

    def one(k):
        to = lax.rem(near + k, 16)
        return remote(part.at[to], r1.at[k], ss.at[0], rs.at[0], near_dev(to))

    def two(k):
        to = lax.rem(far + k, 16)
        return remote(s1, r2.at[k], ss.at[1], rs.at[1], far_dev(to))

    def three(k):
        to = lax.rem(near + k, 16)
        return remote(s2, r3.at[k], ss.at[2], rs.at[2], near_dev(to))

    def all_in(ref, stage):
        every = ref.at[pl.ds(1, 15)]
        remote(every, every, ss.at[stage], rs.at[stage], (dp, fs)).wait()

    def ordered(ref, mine):
        def step(i, total):
            return total + ref[lax.rem(mine - i + 16, 16)]

        return lax.fori_loop(0, 16, step, jnp.zeros((24, 128), F32))

    def gin_tile(which, n):
        start = pl.multiple_of(which * DSH, DSH)
        total = jnp.zeros((DSH, 256), F32)
        for g in range(4):
            total += tn(nall[g, :, pl.ds(start, DSH)], pgrad[g, :, pl.ds(n * 256, 256)])
        return total.astype(BF16)

    spread(one, 0)
    for n in range(6):
        give[:, n * 256 : (n + 1) * 256] = gin_tile(fs, n)
    halves = [pl.ds(pl.multiple_of(g * FSH, FSH), FSH) for g in (f, fo)]
    swaps = [
        remote(give.at[:, pl.ds(i * FSH, FSH)], gin.at[:, halves[i]], gs.at[i], gr.at[i], (dp, fs)) for i in range(2)
    ]
    for swap in swaps:
        swap.start()
    r1[0] = part[near]
    all_in(r1, 0)
    s1[...] = ordered(r1, near)
    spread(two, 1)
    for n in range(6):
        base = pl.multiple_of((f if n < 3 else fo) * FSH + (n % 3) * 256, 256)
        gin[:, pl.ds(base, 256)] = gin_tile(f, n)
    r2[0] = s1[...]
    all_in(r2, 1)
    s2[...] = ordered(r2, far)
    spread(three, 2)

    def gout_tile(n, carry):
        w = pl.ds(pl.multiple_of(n * 256, 256), 256)
        total = jnp.zeros((FSH, 256), F32)
        for g in range(4):
            total += tn(hidden[g, :, pl.ds(0, FSH)], masked[g, :, w])
        gout[:, w] = (0.5 * total).astype(BF16)
        return carry

    lax.fori_loop(0, 6, gout_tile, 0)
    r3[0] = s2[...]
    all_in(r3, 2)

    def lay(k, carry):
        ktot[lax.rem(near - k + 16, 16)] = r3[k] * (1.0 / ROWS)
        return carry

    lax.fori_loop(0, 16, lay, 0)
    sib_halves = [pl.ds(pl.multiple_of(g * FSH, FSH), FSH) for g in (fs, (1 - yh) * 2 + 1 - c)]
    for i, swap in enumerate(swaps):
        swap.wait_send()
        got = gin.at[:, sib_halves[i]]
        remote(got, got, gs.at[i], gr.at[i], (dp, fs)).wait_recv()


def last(part, nall, pgrad, hidden, masked):
    slots = pltpu.VMEM((16, 24, 128), F32)
    one = pltpu.VMEM((24, 128), F32)
    return pl.pallas_call(
        last_kernel,
        out_shape=[
            jax.ShapeDtypeStruct((DSH, FF), BF16),
            jax.ShapeDtypeStruct((FSH, D), BF16),
            jax.ShapeDtypeStruct((16, 24, 128), F32),
        ],
        in_specs=[VM] * 5,
        out_specs=[VM] * 3,
        scratch_shapes=[
            slots, one, slots, one, slots,
            pltpu.VMEM((DSH, HALF), BF16),
            pltpu.SemaphoreType.DMA((3,)),
            pltpu.SemaphoreType.DMA((3,)),
            pltpu.SemaphoreType.DMA((2,)),
            pltpu.SemaphoreType.DMA((2,)),
        ],
        compiler_params=pltpu.CompilerParams(collective_id=4, has_side_effects=True, vmem_limit_bytes=VLIM),
        name="last",
    )(part, nall, pgrad, hidden, masked)


def on_device(
    frames, occupied_slot_counts, block_frame_rows, order, cotangent, sub_weight, depth_kernel, norm_gain, w_in, w_out
):
    dp, f, x, yl, z, yh, c = place()
    mine = jnp.concatenate(
        [block_frame_rows[0, 0], occupied_slot_counts[0], jnp.zeros((15,), jnp.int32), order[0]]
    ).reshape(1, 1, 128)
    table = group_table(mine).reshape(4, NDP, 128)
    peers = jnp.arange(NDP, dtype=jnp.int32)
    origin = (dp - peers) % NDP
    counts, ranking = table[:, :, 48], table[:, 0, 64:]
    earlier = origin[:, None] > origin[None, :]
    starts = jnp.sum(jnp.where(earlier[None], counts[:, None, :], 0), axis=2)
    ends = starts + counts
    first = jnp.sum(jnp.where(ranking == dp, peers[None], 0), axis=1)
    wanted = first[:, None] + NDP * jnp.arange(NB, dtype=jnp.int32)[None]
    from_here = (starts[:, None, :] <= wanted[:, :, None]) & (wanted[:, :, None] < ends[:, None, :])
    slot = jnp.sum(jnp.where(from_here, peers, 0), axis=2)
    within = wanted - jnp.sum(jnp.where(from_here, starts[:, None, :], 0), axis=2)
    row_table = jnp.sum(jnp.where(from_here[..., None], table[:, None, :, :NH], 0), axis=2)
    is_slot = within[:, :, None] == jnp.arange(NH, dtype=jnp.int32)
    valid_rows = jnp.sum(jnp.where(is_slot, row_table, 0), axis=2)
    own_rank, own_start = order[0], lax.dynamic_slice(starts, (f, 0), (1, 1))[0, 0]
    residue = jnp.sum(jnp.where(own_rank[None, :] == peers[:, None], peers[None, :], 0), axis=1)
    hsel = jnp.minimum((residue - own_start) % NDP, NH - 1)
    slot_mine = lax.dynamic_index_in_dim(slot, f, 0, keepdims=False)
    relative = jnp.stack([f, (1 - yh) * 2 + c, yh * 2 + 1 - c, (1 - yh) * 2 + 1 - c])
    rel_rows = jnp.sum(
        jnp.where((relative[:, None] == jnp.arange(4))[..., None], valid_rows[None], 0), axis=1
    )
    masks = (
        (jnp.arange(BR, dtype=jnp.int32)[None, :, None] < rel_rows[:, None, :]).astype(F32).reshape(4, ROWS, 1)
    )
    blocks, cots, winh, wouth, suba, _ = move(
        hsel, slot_mine, frames[0, 0], cotangent[0, 0].reshape(ROWS, D), w_in, w_out, sub_weight
    )
    gain = norm_gain.reshape(1, D)
    masked, feat, conv, normed = front(blocks, suba, cots, masks, depth_kernel, gain)
    nall, pgrad, hidden, ngrad = middle(normed, masked, winh, wouth)
    part = tap_terms(ngrad, masked, feat, conv, masks, gain).reshape(16, 24, 128)
    gin, gout, total = last(part, nall, pgrad, hidden, masked)
    return gin[None], gout[None], total.reshape(D // 128, K + 1, 128).transpose(1, 0, 2).reshape(K + 1, D)[:K]


def solution(mesh):
    placed = (
        P("dp", "fsdp", None, None, None),
        P("fsdp", "dp"),
        P("dp", "fsdp", None),
        P("fsdp", None),
        P("dp", "fsdp", None, None, None),
        P("fsdp", None),
        P(),
        P(),
        P("fsdp", None),
        P("fsdp", None),
    )
    return jax.shard_map(
        on_device,
        mesh=mesh,
        in_specs=placed,
        out_specs=(P("dp", "fsdp", None), P("dp", "fsdp", None), P()),
        check_vma=False,
    )
```

```python
import functools

import jax
import jax.numpy as jnp
from jax import lax
from jax.experimental import pallas as pl
from jax.experimental.pallas import tpu as pltpu
from jax.sharding import PartitionSpec as P

D = 1536
FF = 3072
K = 31
BR = 16
NB = 16
NH = 48
NDP = 64
ROWS = NB * BR
HALF = FF // 2
FSH = FF // 4
DSH = D // 4
SSH = 128
EPSILON = 1e-05
MESH = pl.DeviceIdType.MESH
F32 = jnp.float32
BF16 = jnp.bfloat16
VLIM = 62 * 1024 * 1024
LANES = 128

ANY = pl.BlockSpec(memory_space=pl.ANY)
VM = pl.BlockSpec(memory_space=pltpu.VMEM)
SM = pl.BlockSpec(memory_space=pltpu.SMEM)


def place():
    dp, f = lax.axis_index("dp"), lax.axis_index("fsdp")
    return dp, f, dp // 16, (dp // 8) % 2, dp % 8, f // 2, f % 2


def dev(x, yl, z, yh, c):
    return ((x * 2 + yl) * 8 + z, yh * 2 + c)


def greet(peers, extra=0):
    bar = pltpu.get_barrier_semaphore()
    for peer in peers:
        pl.semaphore_signal(bar, inc=1, device_id=peer, device_id_type=MESH)
    pl.semaphore_wait(bar, len(peers) + extra)


def remote(src, dst, send, recv, device):
    return pltpu.make_async_remote_copy(
        src_ref=src, dst_ref=dst, send_sem=send, recv_sem=recv, device_id=device, device_id_type=MESH
    )


class Sent:
    def __init__(self, src, dst, ss, rs, i, device):
        self.sems, self.device = (ss.at[i], rs.at[i]), device
        self.copy = remote(src, dst, *self.sems, device)

    def start(self):
        self.copy.start()

    def wait(self):
        self.copy.wait()

    def wait_send(self):
        self.copy.wait_send()

    def wait_got(self, ref):
        remote(ref, ref, *self.sems, self.device).wait_recv()


def nt(left, right):
    return lax.dot_general(left, right, (((1,), (1,)), ((), ())), preferred_element_type=F32)


def tn(left, right):
    return lax.dot_general(left, right, (((0,), (0,)), ((), ())), preferred_element_type=F32)


def lane(start, size):
    return pl.ds(pl.multiple_of(start, LANES), size)


def rows(start, size):
    return pl.ds(pl.multiple_of(start, 16), size)


def kernel(
    inv, mine, frames, taps, gain, cot, w_in, w_out, sub,
    gin, gout, ktot,
    table, stab, ends, sbuf, rbuf, blocks, rowv, cots, masked, winv, woutv, suba, stage,
    hgr, nall, pgrad, hidden, picks, patch, maskv, texp, fch, feat, conv, mix, ngrad, part, got,
    tapp, sums, r1, s1, r2, s2, r3,
    ts, tr, as_, ar, ss, rs, ls, gs, gr,
):
    dp, f, x, yl, z, yh, c = place()
    y = yh * 2 + yl
    fs, fo, fso = yh * 2 + 1 - c, (1 - yh) * 2 + c, (1 - yh) * 2 + 1 - c
    color = lax.rem(x + 2 * z, 4)
    across, mate = dev(x, 1 - yl, z, 1 - yh, c), dev(x, 1 - yl, z, yh, c)
    sibling, other, diagonal = (dp, fs), (dp, fo), (dp, fso)
    xp, xm = dev(lax.rem(x + 1, 4), yl, z, yh, c), dev(lax.rem(x + 3, 4), yl, z, yh, c)
    zp, zm = dev(x, yl, lax.rem(z + 1, 8), yh, c), dev(x, yl, lax.rem(z + 7, 8), yh, c)
    near, far = z * 2 + c, x * 4 + y

    def near_dev(i):
        return dev(x, yl, i // 2, yh, lax.rem(i, 2))

    def far_dev(i):
        return dev(i // 4, lax.rem(i, 2), z, lax.rem(i, 4) // 2, c)

    bar = pltpu.get_barrier_semaphore()

    def signal(k, carry):
        pl.semaphore_signal(bar, inc=1, device_id=(lax.rem(dp + k, NDP), f), device_id_type=MESH)
        return carry

    def signal_near(k, carry):
        pl.semaphore_signal(bar, inc=1, device_id=near_dev(lax.rem(near + k, 16)), device_id_type=MESH)
        pl.semaphore_signal(bar, inc=1, device_id=far_dev(lax.rem(far + k, 16)), device_id_type=MESH)
        return carry

    lax.fori_loop(1, NDP, signal, 0)
    lax.fori_loop(1, 16, signal_near, 0)
    greet([across, sibling, other, diagonal], NDP - 1 + 30)

    count = iter(range(64))

    def rcopy(src, dst, device):
        return Sent(src, dst, ss, rs, next(count), device)

    def cols(g):
        return lane(g * FSH, FSH)

    lo, hi = pl.ds(0, FSH), pl.ds(FSH, FSH)

    table[0] = mine[0]

    def send_table(k, carry):
        remote(mine.at[pl.ds(0, 1)], table.at[pl.ds(k, 1)], ts, tr, (lax.rem(dp + k, NDP), f)).start()
        return carry

    lax.fori_loop(1, NDP, send_table, 0)

    def eighth(size):
        return color * 2 * size + yl * size

    q = rows(eighth(48), 48)
    qd = rows(f * DSH + eighth(48), 48)
    qx = rows(color * 96 + (1 - yl) * 48, 48)
    qxd = rows(f * DSH + color * 96 + (1 - yl) * 48, 48)
    sx = rows(color * 32 + (1 - yl) * 16, 16)
    sxd = rows(f * SSH + color * 32 + (1 - yl) * 16, 16)
    ox = rows(color * 192 + (1 - yl) * 96, 96)
    oxd = rows(FSH + color * 192 + (1 - yl) * 96, 96)
    y_sub = [rcopy(sub.at[sx], suba.at[sxd], across)]
    y_out = [rcopy(w_out.at[ox], woutv.at[oxd], across)]
    y_in = [
        rcopy(w_in.at[qx, cols(fo)], winv.at[qxd, lo], across),
        rcopy(w_in.at[qx, cols(f)], winv.at[qxd, hi], across),
        rcopy(w_in.at[qx, cols(fso)], stage.at[qx, lo], across),
        rcopy(w_in.at[qx, cols(fs)], stage.at[qx, hi], across),
    ]
    for copy in y_sub + y_out + y_in:
        copy.start()
    own = rows(f * DSH, DSH)
    on_chip = [
        rcopy(sub, suba.at[rows(f * SSH, SSH)], sibling),
        rcopy(cot, cots.at[1], sibling),
        rcopy(w_in.at[:, cols(fs)], winv.at[own, lo], sibling),
        rcopy(w_in.at[:, cols(fso)], winv.at[own, hi], sibling),
    ]
    local = [
        pltpu.make_async_copy(cot, cots.at[0], ls.at[0]),
        pltpu.make_async_copy(sub, suba.at[rows(f * SSH, SSH)], ls.at[1]),
        pltpu.make_async_copy(w_out, woutv.at[pl.ds(0, FSH)], ls.at[2]),
        pltpu.make_async_copy(w_in.at[:, cols(f)], winv.at[own, lo], ls.at[3]),
        pltpu.make_async_copy(w_in.at[:, cols(fo)], winv.at[own, hi], ls.at[4]),
    ]
    for copy in on_chip + local:
        copy.start()

    rest = table.at[pl.ds(1, NDP - 1)]
    remote(rest, rest, ts, tr, other).wait()
    to_scalar = pltpu.make_async_copy(table, stab, ls.at[5])
    to_scalar.start()
    to_scalar.wait()

    def running(i, total):
        total = total + stab[lax.rem(dp - i + NDP, NDP), 0, NH]
        ends[i] = total
        return total

    lax.fori_loop(0, NDP, running, 0)
    start = ends[dp] - stab[0, 0, NH]

    def pack(j, carry):
        sbuf[j] = frames[jnp.minimum(lax.rem(inv[j] - start + NDP * NH, NDP), NH - 1)]
        return carry

    lax.fori_loop(0, NDP, pack, 0)

    def send(k, carry):
        to = lax.rem(dp + k, NDP)
        remote(sbuf.at[to], rbuf.at[k], as_, ar, (to, f)).start()
        return carry

    lax.fori_loop(1, NDP, send, 0)
    rbuf[0] = sbuf[dp]

    def to_mate(ref, start, size):
        got_rows = rows(start + eighth(size), size)
        copy = rcopy(ref.at[got_rows], ref.at[got_rows], mate)
        copy.start()
        return copy, ref.at[rows(start + color * 2 * size + (1 - yl) * size, size)]

    def from_mate(pair):
        copy, ref = pair
        copy.wait_send()
        copy.wait_got(ref)

    def forward(ref, start, size):
        a = start + color * size
        full, first, second = rows(a, size), rows(a, size // 2), rows(a + size // 2, size // 2)
        copies = [
            rcopy(ref.at[full], ref.at[full], xp),
            rcopy(ref.at[full], ref.at[full], xm),
            rcopy(ref.at[first], ref.at[first], zp),
            rcopy(ref.at[second], ref.at[second], zm),
        ]
        for copy in copies:
            copy.start()
        left, right = start + lax.rem(color + 3, 4) * size, start + lax.rem(color + 1, 4) * size
        beyond = start + lax.rem(color + 2, 4) * size
        spots = [rows(left, size), rows(right, size), rows(beyond, size // 2), rows(beyond + size // 2, size // 2)]
        return [(copy, ref.at[spot]) for copy, spot in zip(copies, spots)]

    def settle(pairs):
        for copy, ref in pairs:
            copy.wait_send()
        for copy, ref in pairs:
            copy.wait_got(ref)

    y_sub[0].wait_send()
    y_sub[0].wait_got(suba.at[rows(fo * SSH + eighth(16), 16)])
    mate_sub = to_mate(suba, fo * SSH, 16)
    y_out[0].wait_send()
    y_out[0].wait_got(woutv.at[rows(FSH + eighth(96), 96)])
    mate_out = to_mate(woutv, FSH, 96)
    from_mate(mate_sub)
    all_sub = forward(suba, fo * SSH, 32)
    for copy in y_in:
        copy.wait_send()
    qi = rows(fo * DSH + eighth(48), 48)
    for copy, ref in zip(y_in, [winv.at[qi, lo], winv.at[qi, hi], stage.at[q, lo], stage.at[q, hi]]):
        copy.wait_got(ref)
    mate_in, mate_stage = to_mate(winv, fo * DSH, 48), to_mate(stage, 0, 48)
    cot_other = rcopy(cot, cots.at[2], other)
    cot_other.start()
    from_mate(mate_out)
    all_out = forward(woutv, FSH, 192)
    from_mate(mate_in)
    all_in_w = forward(winv, fo * DSH, 96)
    from_mate(mate_stage)
    all_stage = forward(stage, 0, 96)

    r = lax.broadcasted_iota(jnp.int32, (ROWS, 4 * ROWS), 0)
    col = lax.broadcasted_iota(jnp.int32, (ROWS, 4 * ROWS), 1)
    want = lax.rem(r, NB) * (4 * BR) + 4 * (r // NB)
    for k in range(4):
        picks[k] = jnp.where(col == want + k, 1.0, 0.0).astype(BF16)

    def turned(g):
        r = lax.broadcasted_iota(jnp.int32, (ROWS, ROWS), 0)
        col = lax.broadcasted_iota(jnp.int32, (ROWS, ROWS), 1)
        turn = jnp.where(col == lax.rem(r, NB) * BR + r // NB, 1.0, 0.0).astype(BF16)
        return jnp.dot(turn, cots[g], preferred_element_type=F32).astype(BF16)

    def hidden_grads(p):
        span = pl.ds(p * 2 * ROWS, 2 * ROWS)

        def tile(n, carry):
            w = lane(n * 256, 256)
            hgr[span, w] = 0.5 * nt(masked[span, :], woutv[w, :])
            return carry

        lax.fori_loop(0, HALF // 256, tile, 0)

    local[0].wait()
    masked[pl.ds(0, ROWS), :] = turned(0)
    on_chip[1].wait()
    masked[pl.ds(ROWS, ROWS), :] = turned(1)
    settle(all_out)
    local[2].wait()
    hidden_grads(0)

    every = rbuf.at[pl.ds(1, NDP - 1)]
    remote(every, every, as_, ar, other).wait()
    first = inv[dp]

    def select(m, height):
        wanted = first + NDP * m
        at = 0
        for step in (32, 16, 8, 4, 2, 1):
            at = jnp.where(ends[at + step - 1] <= wanted, at + step, at)
        slot = lax.rem(dp - at + NDP, NDP)
        blocks[m] = rbuf[slot]
        within = jnp.clip(wanted - (ends[at] - stab[slot, 0, NH]), 0, NH - 1)
        spot = lax.broadcasted_iota(jnp.int32, (NB, LANES), 0)
        return jnp.where(spot == m, stab[slot, 0, within], height)

    rowv[0] = lax.fori_loop(0, NB, select, jnp.zeros((NB, LANES), jnp.int32))
    here = [
        rcopy(rowv.at[0], rowv.at[1], sibling),
        rcopy(rowv.at[0], rowv.at[2], other),
        rcopy(rowv.at[0], rowv.at[3], diagonal),
        rcopy(blocks.at[pl.ds(0, NB)], blocks.at[pl.ds(NB, NB)], other),
    ]
    for copy in here:
        copy.start()
    settle(all_sub)
    theirs = suba.at[rows(fo * SSH, SSH)]
    sub_sib = rcopy(theirs, theirs, sibling)
    sub_sib.start()
    cot_other.wait()
    cot_sib = rcopy(cots.at[2], cots.at[3], sibling)
    cot_sib.start()
    settle(all_stage)
    stage_sib = rcopy(stage, winv.at[rows(fo * DSH, DSH)], sibling)
    stage_sib.start()
    local[1].wait()
    on_chip[0].wait_send()
    on_chip[0].wait_got(suba.at[rows(fs * SSH, SSH)])
    sub_sib.wait_send()
    sub_sib.wait_got(suba.at[rows(fso * SSH, SSH)])

    def fill_mask(g):
        for t in range(BR):
            maskv[g, pl.ds(t * NB, NB), :] = jnp.where(rowv[g] > t, 1.0, 0.0)

    def front(b, g, row):
        fill_mask(g)
        x_in = blocks[pl.ds(b * NB, NB)].reshape(4 * ROWS, LANES)
        for k in range(4):
            patch[:, pl.ds(k * LANES, LANES)] = jnp.dot(picks[k], x_in, preferred_element_type=F32).astype(BF16)

        def project(n, carry):
            w = lane(n * 256, 256)
            total = jnp.dot(patch[...], suba[:, w], preferred_element_type=F32)
            feat[b, :, w] = (total * maskv[g, :, pl.ds(0, 1)]).astype(BF16)
            return carry

        lax.fori_loop(0, D // 256, project, 0)

        def chunk(l, carry):
            w = lane(l * LANES, LANES)
            for k in range(K):
                texp[pl.ds((K - 1 - k) * NB, NB), :] = jnp.broadcast_to(taps[pl.ds(k, 1), w], (NB, LANES))
            fch[...] = feat[b, :, w].astype(F32)
            total = jnp.zeros((BR, NB, LANES), F32)
            for s in range(BR):
                weights = texp[pl.ds((15 - s) * NB, ROWS), :].reshape(BR, NB, LANES)
                total += weights * fch[pl.ds(s * NB, NB), :][None]
            total = total.reshape(ROWS, LANES)
            if b == 0:
                conv[:, w] = total
            mix[:, w] = fch[...] + maskv[g] * (total * jax.nn.sigmoid(total))
            return carry

        lax.fori_loop(0, D // LANES, chunk, 0)

        def norm(i, carry):
            mixed = mix[rows(i * 64, 64), :]
            mean = jnp.mean(mixed, axis=-1, keepdims=True)
            centred = mixed - mean
            variance = jnp.mean(centred * centred, axis=-1, keepdims=True)
            nall[rows(row + i * 64, 64), :] = (centred * lax.rsqrt(variance + EPSILON) * gain[...]).astype(BF16)
            return carry

        lax.fori_loop(0, ROWS // 64, norm, 0)

    front(0, 0, 0)
    norm_swap = rcopy(nall.at[pl.ds(0, ROWS)], nall.at[pl.ds(ROWS, ROWS)], sibling)
    norm_swap.start()

    settle(all_in_w)
    local[3].wait()
    local[4].wait()
    for i, half in ((2, lo), (3, hi)):
        on_chip[i].wait_send()
        on_chip[i].wait_got(winv.at[rows(fs * DSH, DSH), half])
    stage_sib.wait_send()
    stage_sib.wait_got(winv.at[rows(fso * DSH, DSH)])

    def group(p):
        span = pl.ds(p * 2 * ROWS, 2 * ROWS)

        def tile(n, carry):
            w = lane(n * 256, 256)
            pre = jnp.dot(nall[span, :], winv[:, w], preferred_element_type=F32)
            sig = jax.nn.sigmoid(pre)
            hidden[span, w] = (pre * sig).astype(BF16)
            mask = jnp.concatenate([maskv[2 * p], maskv[2 * p + 1]], axis=0)[:, :1]
            pgrad[span, w] = (mask * hgr[span, w] * (sig * (1.0 + pre * (1.0 - sig)))).astype(BF16)
            return carry

        lax.fori_loop(0, HALF // 256, tile, 0)

    def back(g, ref):
        def tile(n, carry):
            w = lane(n * 256, 256)
            ref[:, w] = nt(pgrad[pl.ds(g * ROWS, ROWS), :], winv[w, :])
            return carry

        lax.fori_loop(0, D // 256, tile, 0)

    here[0].wait()
    fill_mask(1)
    norm_swap.wait()
    group(0)
    back(1, part)
    give = rcopy(part, got, sibling)
    give.start()
    back(0, ngrad)
    give.wait()

    def norm_back(i, carry):
        span = rows(i * 64, 64)
        mask = maskv[0, span, :][:, :1]
        pre = conv[span, :]
        sig = jax.nn.sigmoid(pre)
        mixed = feat[0, span, :].astype(F32) + mask * (pre * sig)
        mean = jnp.mean(mixed, axis=-1, keepdims=True)
        centred = mixed - mean
        scale = lax.rsqrt(jnp.mean(centred * centred, axis=-1, keepdims=True) + EPSILON)
        hat = centred * scale
        dn = (ngrad[span, :] + got[span, :]) * gain[...]
        m1 = jnp.mean(dn, axis=-1, keepdims=True)
        m2 = jnp.mean(dn * hat, axis=-1, keepdims=True)
        total = mask * masked[span, :].astype(F32) + scale * (dn - m1 - hat * m2)
        mix[span, :] = mask * total * (sig * (1.0 + pre * (1.0 - sig)))
        return carry

    lax.fori_loop(0, ROWS // 64, norm_back, 0)

    def tap_chunk(l, carry):
        w = lane(l * LANES, LANES)
        fch[...] = feat[0, :, w].astype(F32)
        for k in range(K):
            t0, t1 = max(0, 15 - k), min(BR, 31 - k)
            size = (t1 - t0) * NB
            term = mix[pl.ds(t0 * NB, size), w] * fch[pl.ds((t0 + k - 15) * NB, size), :]
            sums[pl.ds(k, 1), :] = jnp.sum(term, axis=0, keepdims=True)
        sums[pl.ds(K, 1), :] = jnp.zeros((1, LANES), F32)
        tapp[pl.ds(pl.multiple_of(l * (K + 1), 8), K + 1), :] = sums[...]
        return carry

    lax.fori_loop(0, D // LANES, tap_chunk, 0)

    def spread(make):
        def step(k, carry):
            make(k).start()
            return carry

        lax.fori_loop(1, 16, step, 0)

    def rows24(i):
        return pl.ds(pl.multiple_of(i * 24, 8), 24)

    def one(k):
        to = lax.rem(near + k, 16)
        return remote(tapp.at[rows24(to)], r1.at[k], gs.at[0], gr.at[0], near_dev(to))

    def two(k):
        to = lax.rem(far + k, 16)
        return remote(s1, r2.at[k], gs.at[1], gr.at[1], far_dev(to))

    def three(k):
        to = lax.rem(near + k, 16)
        return remote(s2, r3.at[k], gs.at[2], gr.at[2], near_dev(to))

    def all_here(ref, stage_no):
        every = ref.at[pl.ds(1, 15)]
        remote(every, every, gs.at[stage_no], gr.at[stage_no], sibling).wait()

    def ordered(ref, mine_at):
        def step(i, total):
            return total + ref[lax.rem(mine_at - i + 16, 16)]

        return lax.fori_loop(0, 16, step, jnp.zeros((24, LANES), F32))

    spread(one)
    cot_sib.wait()
    masked[pl.ds(2 * ROWS, ROWS), :] = turned(2)
    masked[pl.ds(3 * ROWS, ROWS), :] = turned(3)
    hidden_grads(1)
    here[1].wait()
    here[3].wait()
    front(1, 2, 2 * ROWS)
    norm_swap2 = rcopy(nall.at[pl.ds(2 * ROWS, ROWS)], nall.at[pl.ds(3 * ROWS, ROWS)], sibling)
    norm_swap2.start()
    here[2].wait()
    fill_mask(3)
    r1[0] = tapp[rows24(near), :]
    all_here(r1, 0)
    s1[...] = ordered(r1, near)
    spread(two)
    for g in range(4):
        if g == 2:
            norm_swap2.wait()
            group(1)
        span = pl.ds(g * ROWS, ROWS)
        masked[span, :] = jnp.where(maskv[g][:, :1] > 0, masked[span, :].astype(F32), 0.0).astype(BF16)
    r2[0] = s1[...]
    all_here(r2, 1)
    s2[...] = ordered(r2, far)
    spread(three)

    def gin_tile(which, n):
        return tn(nall[:, lane(which * DSH, DSH)], pgrad[:, lane(n * 256, 256)]).astype(BF16)

    def give_tile(n, carry):
        stage[:, lane(n * 256, 256)] = gin_tile(fs, n)
        return carry

    lax.fori_loop(0, 6, give_tile, 0)
    swaps = [rcopy(stage.at[:, half], gin.at[:, cols(g)], sibling) for half, g in ((lo, f), (hi, fo))]
    for swap in swaps:
        swap.start()

    def keep_tile(n, carry):
        gin[:, lane(f * FSH + n * 256, 256)] = gin_tile(f, n)
        gin[:, lane(fo * FSH + n * 256, 256)] = gin_tile(f, n + 3)
        return carry

    lax.fori_loop(0, 3, keep_tile, 0)

    def gout_tile(n, carry):
        w = lane(n * 256, 256)
        gout[:, w] = (0.5 * tn(hidden[:, pl.ds(0, FSH)], masked[:, w])).astype(BF16)
        return carry

    lax.fori_loop(0, D // 256, gout_tile, 0)
    r3[0] = s2[...]
    all_here(r3, 2)

    def lay(k, carry):
        ktot[lax.rem(near - k + 16, 16)] = r3[k] * (1.0 / ROWS)
        return carry

    lax.fori_loop(0, 16, lay, 0)
    for swap, g in zip(swaps, (fs, fso)):
        swap.wait_send()
        swap.wait_got(gin.at[:, cols(g)])


def on_device(
    frames, occupied_slot_counts, block_frame_rows, order, cotangent, sub_weight, depth_kernel, norm_gain, w_in, w_out
):
    mine = jnp.concatenate(
        [block_frame_rows[0, 0], occupied_slot_counts[0], jnp.zeros((LANES - NH - 1,), jnp.int32)]
    ).reshape(1, 1, LANES)
    peers = jnp.arange(NDP, dtype=jnp.int32)
    inv = jnp.sum(jnp.where(order[0][None, :] == peers[:, None], peers[None, :], 0), axis=1)
    vm, dma = pltpu.VMEM, pltpu.SemaphoreType.DMA
    slots, one = vm((16, 24, LANES), F32), vm((24, LANES), F32)
    gin, gout, total = pl.pallas_call(
        kernel,
        out_shape=[
            jax.ShapeDtypeStruct((DSH, FF), BF16),
            jax.ShapeDtypeStruct((FSH, D), BF16),
            jax.ShapeDtypeStruct((16, 24, LANES), F32),
        ],
        in_specs=[SM, VM, VM, VM, VM, ANY, ANY, ANY, ANY],
        out_specs=[VM] * 3,
        scratch_shapes=[
            vm((NDP, 1, LANES), jnp.int32),
            pltpu.SMEM((NDP, 1, LANES), jnp.int32),
            pltpu.SMEM((NDP,), jnp.int32),
            vm((NDP, 64, LANES), BF16),
            vm((NDP, 64, LANES), BF16),
            vm((2 * NB, 64, LANES), BF16),
            vm((4, NB, LANES), jnp.int32),
            vm((4, ROWS, D), BF16),
            vm((4 * ROWS, D), BF16),
            vm((D, HALF), BF16),
            vm((HALF, D), BF16),
            vm((4 * SSH, D), BF16),
            vm((DSH, HALF), BF16),
            vm((4 * ROWS, HALF), F32),
            vm((4 * ROWS, D), BF16),
            vm((4 * ROWS, HALF), BF16),
            vm((4 * ROWS, HALF), BF16),
            vm((4, ROWS, 4 * ROWS), BF16),
            vm((ROWS, 4 * LANES), BF16),
            vm((4, ROWS, LANES), F32),
            vm((K * NB, LANES), F32),
            vm((ROWS, LANES), F32),
            vm((2, ROWS, D), BF16),
            vm((ROWS, D), F32),
            vm((ROWS, D), F32),
            vm((ROWS, D), F32),
            vm((ROWS, D), F32),
            vm((ROWS, D), F32),
            vm((D // LANES * (K + 1), LANES), F32),
            vm((K + 1, LANES), F32),
            slots, one, slots, one, slots,
            dma, dma, dma, dma,
            dma((48,)), dma((48,)), dma((6,)), dma((3,)), dma((3,)),
        ],
        compiler_params=pltpu.CompilerParams(collective_id=1, has_side_effects=True, vmem_limit_bytes=VLIM),
        name="window",
    )(
        inv, mine, frames[0, 0], depth_kernel, norm_gain.reshape(1, D),
        cotangent[0, 0].reshape(ROWS, D), w_in, w_out, sub_weight,
    )
    total = total.reshape(D // LANES, K + 1, LANES).transpose(1, 0, 2).reshape(K + 1, D)
    return gin[None], gout[None], total[:K]


def solution(mesh):
    placed = (
        P("dp", "fsdp", None, None, None),
        P("fsdp", "dp"),
        P("dp", "fsdp", None),
        P("fsdp", None),
        P("dp", "fsdp", None, None, None),
        P("fsdp", None),
        P(),
        P(),
        P("fsdp", None),
        P("fsdp", None),
    )
    return jax.shard_map(
        on_device,
        mesh=mesh,
        in_specs=placed,
        out_specs=(P("dp", "fsdp", None), P("dp", "fsdp", None), P()),
        check_vma=False,
    )
```

```python
import functools

import jax
import jax.numpy as jnp
from jax import lax
from jax.experimental import pallas as pl
from jax.experimental.pallas import tpu as pltpu
from jax.sharding import PartitionSpec as P

D = 1536
FF = 3072
K = 31
BR = 16
NB = 16
NH = 48
NDP = 64
ROWS = NB * BR
HALF = FF // 2
FSH = FF // 4
DSH = D // 4
SSH = 128
EPSILON = 1e-05
MESH = pl.DeviceIdType.MESH
F32 = jnp.float32
BF16 = jnp.bfloat16
VLIM = 62 * 1024 * 1024
LANES = 128

ANY = pl.BlockSpec(memory_space=pl.ANY)
VM = pl.BlockSpec(memory_space=pltpu.VMEM)
SM = pl.BlockSpec(memory_space=pltpu.SMEM)


def place():
    dp, f = lax.axis_index("dp"), lax.axis_index("fsdp")
    return dp, f, dp // 16, (dp // 8) % 2, dp % 8, f // 2, f % 2


def dev(x, yl, z, yh, c):
    return ((x * 2 + yl) * 8 + z, yh * 2 + c)


def greet(peers, extra=0):
    bar = pltpu.get_barrier_semaphore()
    for peer in peers:
        pl.semaphore_signal(bar, inc=1, device_id=peer, device_id_type=MESH)
    pl.semaphore_wait(bar, len(peers) + extra)


def remote(src, dst, send, recv, device):
    return pltpu.make_async_remote_copy(
        src_ref=src, dst_ref=dst, send_sem=send, recv_sem=recv, device_id=device, device_id_type=MESH
    )


class Sent:
    def __init__(self, src, dst, ss, rs, i, device):
        self.sems, self.device = (ss.at[i], rs.at[i]), device
        self.copy = remote(src, dst, *self.sems, device)

    def start(self):
        self.copy.start()

    def wait(self):
        self.copy.wait()

    def wait_send(self):
        self.copy.wait_send()

    def wait_got(self, ref):
        remote(ref, ref, *self.sems, self.device).wait_recv()


def nt(left, right):
    return lax.dot_general(left, right, (((1,), (1,)), ((), ())), preferred_element_type=F32)


def tn(left, right):
    return lax.dot_general(left, right, (((0,), (0,)), ((), ())), preferred_element_type=F32)


def lane(start, size):
    return pl.ds(pl.multiple_of(start, LANES), size)


def rows(start, size):
    return pl.ds(pl.multiple_of(start, 16), size)


def kernel(
    count_in, rows_in, order_in, frames_hbm, taps, gain, cot, w_in, w_out, sub,
    gin, gout, ktot,
    frames, ginv, goutv, mine, invv, inv, slots, table, stab, ends, sbuf, rbuf, blocks, rowv, cots, masked, winv, woutv, suba, stage,
    hgr, nall, pgrad, hidden, picks, patch, maskv, texp, fch, feat, conv, mix, ngrad, part, got,
    tapp, sums, r1, s1, r2, s2, r3,
    ts, tr, as_, ar, ss, rs, ls, gs, gr, ps, pr, os_,
):
    dp, f, x, yl, z, yh, c = place()
    y = yh * 2 + yl
    fs, fo, fso = yh * 2 + 1 - c, (1 - yh) * 2 + c, (1 - yh) * 2 + 1 - c
    color = lax.rem(x + 2 * z, 4)
    across, mate = dev(x, 1 - yl, z, 1 - yh, c), dev(x, 1 - yl, z, yh, c)
    sibling, other, diagonal = (dp, fs), (dp, fo), (dp, fso)
    xp, xm = dev(lax.rem(x + 1, 4), yl, z, yh, c), dev(lax.rem(x + 3, 4), yl, z, yh, c)
    zp, zm = dev(x, yl, lax.rem(z + 1, 8), yh, c), dev(x, yl, lax.rem(z + 7, 8), yh, c)
    near, far = z * 2 + c, x * 4 + y

    def near_dev(i):
        return dev(x, yl, i // 2, yh, lax.rem(i, 2))

    def far_dev(i):
        return dev(i // 4, lax.rem(i, 2), z, lax.rem(i, 4) // 2, c)

    frames_in = pltpu.make_async_copy(frames_hbm, frames, ls.at[5])
    frames_in.start()
    mine[0] = jnp.full((1, LANES), count_in[0, 0], jnp.int32)
    mine[0, :, pl.ds(0, NH)] = rows_in[...]
    bar = pltpu.get_barrier_semaphore()

    def signal(k, carry):
        pl.semaphore_signal(bar, inc=1, device_id=(lax.rem(dp + k, NDP), f), device_id_type=MESH)
        return carry

    def signal_near(k, carry):
        zz, xy = lax.rem(z + k, 8), lax.rem(x * 2 + yl + k, 8)
        pl.semaphore_signal(bar, inc=1, device_id=dev(x, yl, zz, yh, 1 - c), device_id_type=MESH)
        pl.semaphore_signal(bar, inc=1, device_id=dev(xy // 2, lax.rem(xy, 2), z, 1 - yh, c), device_id_type=MESH)
        return carry

    lax.fori_loop(1, NDP, signal, 0)
    lax.fori_loop(1, 8, signal_near, 0)
    greet([sibling, other, diagonal], NDP - 1 + 14)

    count = iter(range(64))

    def rcopy(src, dst, device):
        return Sent(src, dst, ss, rs, next(count), device)

    def cols(g):
        return lane(g * FSH, FSH)

    lo, hi = pl.ds(0, FSH), pl.ds(FSH, FSH)

    table[0] = mine[0]

    def send_table(k, carry):
        remote(mine.at[pl.ds(0, 1)], table.at[pl.ds(k, 1)], ts, tr, (lax.rem(dp + k, NDP), f)).start()
        return carry

    lax.fori_loop(1, NDP, send_table, 0)
    home = lax.broadcasted_iota(jnp.int32, (NDP, NDP), 0)
    residue = lax.broadcasted_iota(jnp.int32, (NDP, NDP), 1)
    picked = jnp.where(order_in[...] == home, residue, 0)
    invv[...] = jnp.broadcast_to(jnp.sum(picked, axis=1, keepdims=True), (NDP, LANES))
    inv_copy = pltpu.make_async_copy(invv, inv, ls.at[6])
    inv_copy.start()

    def eighth(size):
        return color * 2 * size + yl * size

    q = rows(eighth(48), 48)
    qd = rows(f * DSH + eighth(48), 48)
    qx = rows(color * 96 + (1 - yl) * 48, 48)
    qxd = rows(f * DSH + color * 96 + (1 - yl) * 48, 48)
    sx = rows(color * 32 + (1 - yl) * 16, 16)
    sxd = rows(f * SSH + color * 32 + (1 - yl) * 16, 16)
    ox = rows(color * 192 + (1 - yl) * 96, 96)
    oxd = rows(FSH + color * 192 + (1 - yl) * 96, 96)
    y_sub = [rcopy(sub.at[sx], suba.at[sxd], across)]
    y_out = [rcopy(w_out.at[ox], woutv.at[oxd], across)]
    y_in = [
        rcopy(w_in.at[qx, cols(fo)], winv.at[qxd, lo], across),
        rcopy(w_in.at[qx, cols(f)], winv.at[qxd, hi], across),
        rcopy(w_in.at[qx, cols(fso)], stage.at[qx, lo], across),
        rcopy(w_in.at[qx, cols(fs)], stage.at[qx, hi], across),
    ]
    for copy in y_sub + y_out + y_in:
        copy.start()
    own = rows(f * DSH, DSH)
    on_chip = [
        rcopy(sub, suba.at[rows(f * SSH, SSH)], sibling),
        rcopy(cot, cots.at[1], sibling),
        rcopy(w_in.at[:, cols(fs)], winv.at[own, lo], sibling),
        rcopy(w_in.at[:, cols(fso)], winv.at[own, hi], sibling),
    ]
    local = [
        pltpu.make_async_copy(cot, cots.at[0], ls.at[0]),
        pltpu.make_async_copy(sub, suba.at[rows(f * SSH, SSH)], ls.at[1]),
        pltpu.make_async_copy(w_out, woutv.at[pl.ds(0, FSH)], ls.at[2]),
        pltpu.make_async_copy(w_in.at[:, cols(f)], winv.at[own, lo], ls.at[3]),
        pltpu.make_async_copy(w_in.at[:, cols(fo)], winv.at[own, hi], ls.at[4]),
    ]
    for copy in on_chip + local:
        copy.start()

    def settle(pairs):
        for copy, ref in pairs:
            copy.wait_send()
        for copy, ref in pairs:
            copy.wait_got(ref)

    def eighths(start, size, shift, part_of):
        return rows(start + lax.rem(color + shift, 4) * 2 * size + part_of * size, size)

    def pass_on(ref, start, size):
        here = ref.at[eighths(start, size, 0, yl)]
        copies = [rcopy(here, here, peer) for peer in (mate, xp, xm, zp)]
        for copy in copies:
            copy.start()
        spots = [(0, 1 - yl), (3, yl), (1, yl), (2, yl)]
        return [(copy, ref.at[eighths(start, size, *spot)]) for copy, spot in zip(copies, spots)]

    def pass_mate(ref, start, size, pairs):
        settle(pairs[:1])
        here = ref.at[eighths(start, size, 0, 1 - yl)]
        copies = [rcopy(here, here, peer) for peer in (xp, xm, zm)]
        for copy in copies:
            copy.start()
        spots = [(3, 1 - yl), (1, 1 - yl), (2, 1 - yl)]
        return pairs[1:] + [(copy, ref.at[eighths(start, size, *spot)]) for copy, spot in zip(copies, spots)]

    y_sub[0].wait_send()
    y_sub[0].wait_got(suba.at[rows(fo * SSH + eighth(16), 16)])
    all_sub = pass_on(suba, fo * SSH, 16)

    rest = table.at[pl.ds(1, NDP - 1)]
    remote(rest, rest, ts, tr, other).wait()
    to_scalar = pltpu.make_async_copy(table, stab, ls.at[7])
    to_scalar.start()
    to_scalar.wait()
    inv_copy.wait()
    frames_in.wait()

    def running(i, total):
        total = total + stab[lax.rem(dp - i + NDP, NDP), 0, NH]
        ends[i] = total
        return total

    lax.fori_loop(0, NDP, running, 0)
    start = ends[dp] - stab[0, 0, NH]

    def pick_home(j):
        return frames[jnp.minimum(lax.rem(inv[j, 0] - start + NDP * NH, NDP), NH - 1)]

    def send(k, carry):
        kk = lax.rem(k * 27, NDP)
        to = lax.rem(dp + kk, NDP)
        sbuf[to] = pick_home(to)
        remote(sbuf.at[to], rbuf.at[kk], as_, ar, (to, f)).start()
        return carry

    lax.fori_loop(1, NDP, send, 0)
    rbuf[0] = pick_home(dp)

    y_out[0].wait_send()
    y_out[0].wait_got(woutv.at[rows(FSH + eighth(96), 96)])
    all_out = pass_on(woutv, FSH, 96)
    all_sub = pass_mate(suba, fo * SSH, 16, all_sub)
    for copy in y_in:
        copy.wait_send()
    qi = rows(fo * DSH + eighth(48), 48)
    for copy, ref in zip(y_in, [winv.at[qi, lo], winv.at[qi, hi], stage.at[q, lo], stage.at[q, hi]]):
        copy.wait_got(ref)
    all_stage = pass_on(stage, 0, 48)
    all_in_w = pass_on(winv, fo * DSH, 48)
    all_out = pass_mate(woutv, FSH, 96, all_out)
    all_stage = pass_mate(stage, 0, 48, all_stage)
    all_in_w = pass_mate(winv, fo * DSH, 48, all_in_w)

    first = inv[dp, 0]

    def choose(m, height):
        wanted = first + NDP * m
        at = 0
        for step in (32, 16, 8, 4, 2, 1):
            at = jnp.where(ends[at + step - 1] <= wanted, at + step, at)
        slot = lax.rem(dp - at + NDP, NDP)
        within = jnp.clip(wanted - (ends[at] - stab[slot, 0, NH]), 0, NH - 1)
        slots[m] = slot
        spot = lax.broadcasted_iota(jnp.int32, (NB, LANES), 0)
        return jnp.where(spot == m, stab[slot, 0, within], height)

    rowv[0] = lax.fori_loop(0, NB, choose, jnp.zeros((NB, LANES), jnp.int32))

    r = lax.broadcasted_iota(jnp.int32, (ROWS, 4 * ROWS), 0)
    col = lax.broadcasted_iota(jnp.int32, (ROWS, 4 * ROWS), 1)
    want = lax.rem(r, NB) * (4 * BR) + 4 * (r // NB)
    for k in range(4):
        picks[k] = jnp.where(col == want + k, 1.0, 0.0).astype(BF16)

    def turned(g):
        r = lax.broadcasted_iota(jnp.int32, (ROWS, ROWS), 0)
        col = lax.broadcasted_iota(jnp.int32, (ROWS, ROWS), 1)
        turn = jnp.where(col == lax.rem(r, NB) * BR + r // NB, 1.0, 0.0).astype(BF16)
        return jnp.dot(turn, cots[g], preferred_element_type=F32).astype(BF16)

    def hidden_grads(p):
        span = pl.ds(p * 2 * ROWS, 2 * ROWS)

        def tile(n, carry):
            w = lane(n * 256, 256)
            hgr[span, w] = 0.5 * nt(masked[span, :], woutv[w, :])
            return carry

        lax.fori_loop(0, HALF // 256, tile, 0)

    local[0].wait()
    masked[pl.ds(0, ROWS), :] = turned(0)
    on_chip[1].wait()
    masked[pl.ds(ROWS, ROWS), :] = turned(1)

    every = rbuf.at[pl.ds(1, NDP - 1)]
    remote(every, every, as_, ar, other).wait()

    def select(m, carry):
        blocks[m] = rbuf[slots[m]]
        return carry

    lax.fori_loop(0, NB, select, 0)
    here = [
        rcopy(rowv.at[0], rowv.at[1], sibling),
        rcopy(rowv.at[0], rowv.at[2], other),
        rcopy(rowv.at[0], rowv.at[3], diagonal),
        rcopy(blocks.at[pl.ds(0, NB)], blocks.at[pl.ds(NB, NB)], other),
    ]
    for copy in here:
        copy.start()
    cot_other = rcopy(cot, cots.at[2], other)
    cot_other.start()
    settle(all_sub)
    theirs = suba.at[rows(fo * SSH, SSH)]
    sub_sib = rcopy(theirs, theirs, sibling)
    sub_sib.start()
    settle(all_stage)
    stage_sib = rcopy(stage, winv.at[rows(fo * DSH, DSH)], sibling)
    stage_sib.start()
    local[1].wait()
    on_chip[0].wait_send()
    on_chip[0].wait_got(suba.at[rows(fs * SSH, SSH)])
    sub_sib.wait_send()
    sub_sib.wait_got(suba.at[rows(fso * SSH, SSH)])

    def fill_mask(g):
        for t in range(BR):
            maskv[g, pl.ds(t * NB, NB), :] = jnp.where(rowv[g] > t, 1.0, 0.0)

    def front(b, g, row):
        fill_mask(g)
        x_in = blocks[pl.ds(b * NB, NB)].reshape(4 * ROWS, LANES)
        for k in range(4):
            patch[:, pl.ds(k * LANES, LANES)] = jnp.dot(picks[k], x_in, preferred_element_type=F32).astype(BF16)

        def project(n, carry):
            w = lane(n * 256, 256)
            total = jnp.dot(patch[...], suba[:, w], preferred_element_type=F32)
            feat[b, :, w] = (total * maskv[g, :, pl.ds(0, 1)]).astype(BF16)
            return carry

        lax.fori_loop(0, D // 256, project, 0)

        def chunk(l, carry):
            w = lane(l * LANES, LANES)
            for k in range(K):
                texp[pl.ds((K - 1 - k) * NB, NB), :] = jnp.broadcast_to(taps[pl.ds(k, 1), w], (NB, LANES))
            fch[...] = feat[b, :, w].astype(F32)
            total = jnp.zeros((BR, NB, LANES), F32)
            for s in range(BR):
                weights = texp[pl.ds((15 - s) * NB, ROWS), :].reshape(BR, NB, LANES)
                total += weights * fch[pl.ds(s * NB, NB), :][None]
            total = total.reshape(ROWS, LANES)
            if b == 0:
                conv[:, w] = total
            mix[:, w] = fch[...] + maskv[g] * (total * jax.nn.sigmoid(total))
            return carry

        lax.fori_loop(0, D // LANES, chunk, 0)

        def norm(i, carry):
            mixed = mix[rows(i * 64, 64), :]
            mean = jnp.mean(mixed, axis=-1, keepdims=True)
            centred = mixed - mean
            variance = jnp.mean(centred * centred, axis=-1, keepdims=True)
            nall[rows(row + i * 64, 64), :] = (centred * lax.rsqrt(variance + EPSILON) * gain[...][None, :]).astype(BF16)
            swap = nall.at[rows(row + i * 64, 64)], nall.at[rows(row + ROWS + i * 64, 64)]
            remote(*swap, ps.at[b * 4 + i], pr.at[b * 4 + i], sibling).start()
            return carry

        lax.fori_loop(0, ROWS // 64, norm, 0)

    def norm_here(b, row):
        def step(i, carry):
            swap = nall.at[rows(row + i * 64, 64)], nall.at[rows(row + ROWS + i * 64, 64)]
            remote(*swap, ps.at[b * 4 + i], pr.at[b * 4 + i], sibling).wait()
            return carry

        lax.fori_loop(0, ROWS // 64, step, 0)

    front(0, 0, 0)
    settle(all_out)
    local[2].wait()
    hidden_grads(0)

    settle(all_in_w)
    local[3].wait()
    local[4].wait()
    for i, half in ((2, lo), (3, hi)):
        on_chip[i].wait_send()
        on_chip[i].wait_got(winv.at[rows(fs * DSH, DSH), half])
    stage_sib.wait_send()
    stage_sib.wait_got(winv.at[rows(fso * DSH, DSH)])

    def group(p):
        span = pl.ds(p * 2 * ROWS, 2 * ROWS)

        def tile(n, carry):
            w = lane(n * 256, 256)
            pre = jnp.dot(nall[span, :], winv[:, w], preferred_element_type=F32)
            sig = jax.nn.sigmoid(pre)
            hidden[span, w] = (pre * sig).astype(BF16)
            mask = jnp.concatenate([maskv[2 * p], maskv[2 * p + 1]], axis=0)[:, :1]
            pgrad[span, w] = (mask * hgr[span, w] * (sig * (1.0 + pre * (1.0 - sig)))).astype(BF16)
            return carry

        lax.fori_loop(0, HALF // 256, tile, 0)

    def given(n):
        w = lane(n * 256, 256)
        return remote(part.at[:, w], got.at[:, w], ps.at[8 + n], pr.at[8 + n], sibling)

    def back(g, ref):
        def tile(n, carry):
            w = lane(n * 256, 256)
            ref[:, w] = nt(pgrad[pl.ds(g * ROWS, ROWS), :], winv[w, :])
            if g == 1:
                given(n).start()
            return carry

        lax.fori_loop(0, D // 256, tile, 0)

    here[0].wait()
    fill_mask(1)
    norm_here(0, 0)
    group(0)
    back(1, part)
    back(0, ngrad)

    def take(n, carry):
        given(n).wait()
        return carry

    lax.fori_loop(0, D // 256, take, 0)

    def norm_back(i, carry):
        span = rows(i * 64, 64)
        mask = maskv[0, span, :][:, :1]
        pre = conv[span, :]
        sig = jax.nn.sigmoid(pre)
        mixed = feat[0, span, :].astype(F32) + mask * (pre * sig)
        mean = jnp.mean(mixed, axis=-1, keepdims=True)
        centred = mixed - mean
        scale = lax.rsqrt(jnp.mean(centred * centred, axis=-1, keepdims=True) + EPSILON)
        hat = centred * scale
        dn = (ngrad[span, :] + got[span, :]) * gain[...][None, :]
        m1 = jnp.mean(dn, axis=-1, keepdims=True)
        m2 = jnp.mean(dn * hat, axis=-1, keepdims=True)
        total = mask * masked[span, :].astype(F32) + scale * (dn - m1 - hat * m2)
        mix[span, :] = mask * total * (sig * (1.0 + pre * (1.0 - sig)))
        return carry

    lax.fori_loop(0, ROWS // 64, norm_back, 0)

    def tap_chunk(l, carry):
        w = lane(l * LANES, LANES)
        fch[...] = feat[0, :, w].astype(F32)
        for k in range(K):
            t0, t1 = max(0, 15 - k), min(BR, 31 - k)
            size = (t1 - t0) * NB
            term = mix[pl.ds(t0 * NB, size), w] * fch[pl.ds((t0 + k - 15) * NB, size), :]
            sums[pl.ds(k, 1), :] = jnp.sum(term, axis=0, keepdims=True)
        sums[pl.ds(K, 1), :] = jnp.zeros((1, LANES), F32)
        tapp[pl.ds(pl.multiple_of(l * (K + 1), 8), K + 1), :] = sums[...]
        return carry

    lax.fori_loop(0, D // LANES, tap_chunk, 0)

    def spread(make):
        def step(k, carry):
            make(k).start()
            return carry

        lax.fori_loop(1, 16, step, 0)

    def rows24(i):
        return pl.ds(pl.multiple_of(i * 24, 8), 24)

    def one(k):
        to = lax.rem(near + k, 16)
        return remote(tapp.at[rows24(to)], r1.at[k], gs.at[0], gr.at[0], near_dev(to))

    def two(k):
        to = lax.rem(far + k, 16)
        return remote(s1, r2.at[k], gs.at[1], gr.at[1], far_dev(to))

    def three(k):
        to = lax.rem(near + k, 16)
        return remote(s2, r3.at[k], gs.at[2], gr.at[2], near_dev(to))

    def all_here(ref, stage_no):
        every = ref.at[pl.ds(1, 15)]
        remote(every, every, gs.at[stage_no], gr.at[stage_no], sibling).wait()

    def ordered(ref, mine_at):
        def step(i, total):
            return total + ref[lax.rem(mine_at - i + 16, 16)]

        return lax.fori_loop(0, 16, step, jnp.zeros((24, LANES), F32))

    spread(one)
    here[1].wait()
    here[3].wait()
    front(1, 2, 2 * ROWS)
    here[2].wait()
    fill_mask(3)
    r1[0] = tapp[rows24(near), :]
    all_here(r1, 0)
    s1[...] = ordered(r1, near)
    spread(two)
    cot_other.wait()
    cot_sib = rcopy(cots.at[2], cots.at[3], sibling)
    cot_sib.start()
    masked[pl.ds(2 * ROWS, ROWS), :] = turned(2)
    cot_sib.wait()
    masked[pl.ds(3 * ROWS, ROWS), :] = turned(3)
    hidden_grads(1)
    for g in range(4):
        if g == 2:
            norm_here(1, 2 * ROWS)
            group(1)
        span = pl.ds(g * ROWS, ROWS)
        masked[span, :] = jnp.where(maskv[g][:, :1] > 0, masked[span, :].astype(F32), 0.0).astype(BF16)
    r2[0] = s1[...]
    all_here(r2, 1)
    s2[...] = ordered(r2, far)
    spread(three)

    def gin_tile(which, n):
        return tn(nall[:, lane(which * DSH, DSH)], pgrad[:, lane(n * 256, 256)]).astype(BF16)

    def give_tile(n, carry):
        stage[:, lane(n * 256, 256)] = gin_tile(fs, n)
        return carry

    lax.fori_loop(0, 6, give_tile, 0)
    swaps = [rcopy(stage.at[:, half], ginv.at[:, cols(g)], sibling) for half, g in ((lo, f), (hi, fo))]
    for swap in swaps:
        swap.start()

    def leave(ref, out, w, i):
        return pltpu.make_async_copy(ref.at[:, w], out.at[:, w], os_.at[i])

    def keep_tile(n, carry):
        first, second = lane(f * FSH + n * 256, 256), lane(fo * FSH + n * 256, 256)
        ginv[:, first] = gin_tile(f, n)
        leave(ginv, gin, first, n).start()
        ginv[:, second] = gin_tile(f, n + 3)
        leave(ginv, gin, second, 3 + n).start()
        return carry

    lax.fori_loop(0, 3, keep_tile, 0)

    def gout_tile(n, carry):
        w = lane(n * 256, 256)
        goutv[:, w] = (0.5 * tn(hidden[:, pl.ds(0, FSH)], masked[:, w])).astype(BF16)
        leave(goutv, gout, w, 6 + n).start()
        return carry

    lax.fori_loop(0, D // 256, gout_tile, 0)
    for i, (swap, g) in enumerate(zip(swaps, (fs, fso))):
        swap.wait_send()
        swap.wait_got(ginv.at[:, cols(g)])
        leave(ginv, gin, cols(g), 12 + i).start()
    r3[0] = s2[...]
    all_here(r3, 2)

    def lay(k, carry):
        tapp[rows24(lax.rem(near - k + 16, 16)), :] = r3[k] * (1.0 / ROWS)
        return carry

    lax.fori_loop(0, 16, lay, 0)
    for l in range(D // LANES):
        ktot[:, pl.ds(l * LANES, LANES)] = tapp[pl.ds(l * (K + 1), K), :]

    def gone(n, carry):
        leave(ginv, gin, lane(f * FSH + n * 256, 256), n).wait()
        leave(ginv, gin, lane(fo * FSH + n * 256, 256), 3 + n).wait()
        leave(goutv, gout, lane(n * 256, 256), 6 + n).wait()
        leave(goutv, gout, lane((n + 3) * 256, 256), 9 + n).wait()
        return carry

    lax.fori_loop(0, 3, gone, 0)
    for i, g in enumerate((fs, fso)):
        leave(ginv, gin, cols(g), 12 + i).wait()


def on_device(
    frames, occupied_slot_counts, block_frame_rows, order, cotangent, sub_weight, depth_kernel, norm_gain, w_in, w_out
):
    vm, dma = pltpu.VMEM, pltpu.SemaphoreType.DMA
    stages, one = vm((16, 24, LANES), F32), vm((24, LANES), F32)
    gin, gout, total = pl.pallas_call(
        kernel,
        out_shape=[
            jax.ShapeDtypeStruct((DSH, FF), BF16),
            jax.ShapeDtypeStruct((FSH, D), BF16),
            jax.ShapeDtypeStruct((K, D), F32),
        ],
        in_specs=[SM, VM, VM, ANY, VM, VM, ANY, ANY, ANY, ANY],
        out_specs=[ANY, ANY, VM],
        scratch_shapes=[
            vm((NH, 64, LANES), BF16),
            vm((DSH, FF), BF16),
            vm((FSH, D), BF16),
            vm((1, 1, LANES), jnp.int32),
            vm((NDP, LANES), jnp.int32),
            pltpu.SMEM((NDP, LANES), jnp.int32),
            pltpu.SMEM((NB,), jnp.int32),
            vm((NDP, 1, LANES), jnp.int32),
            pltpu.SMEM((NDP, 1, LANES), jnp.int32),
            pltpu.SMEM((NDP,), jnp.int32),
            vm((NDP, 64, LANES), BF16),
            vm((NDP, 64, LANES), BF16),
            vm((2 * NB, 64, LANES), BF16),
            vm((4, NB, LANES), jnp.int32),
            vm((4, ROWS, D), BF16),
            vm((4 * ROWS, D), BF16),
            vm((D, HALF), BF16),
            vm((HALF, D), BF16),
            vm((4 * SSH, D), BF16),
            vm((DSH, HALF), BF16),
            vm((4 * ROWS, HALF), F32),
            vm((4 * ROWS, D), BF16),
            vm((4 * ROWS, HALF), BF16),
            vm((4 * ROWS, HALF), BF16),
            vm((4, ROWS, 4 * ROWS), BF16),
            vm((ROWS, 4 * LANES), BF16),
            vm((4, ROWS, LANES), F32),
            vm((K * NB, LANES), F32),
            vm((ROWS, LANES), F32),
            vm((2, ROWS, D), BF16),
            vm((ROWS, D), F32),
            vm((ROWS, D), F32),
            vm((ROWS, D), F32),
            vm((ROWS, D), F32),
            vm((ROWS, D), F32),
            vm((D // LANES * (K + 1), LANES), F32),
            vm((K + 1, LANES), F32),
            stages, one, stages, one, stages,
            dma, dma, dma, dma,
            dma((56,)), dma((56,)), dma((8,)), dma((3,)), dma((3,)), dma((14,)), dma((14,)), dma((14,)),
        ],
        compiler_params=pltpu.CompilerParams(collective_id=1, has_side_effects=True, vmem_limit_bytes=VLIM),
        name="window",
    )(
        occupied_slot_counts, block_frame_rows[0], order, frames[0, 0], depth_kernel, norm_gain,
        cotangent[0, 0].reshape(ROWS, D), w_in, w_out, sub_weight,
    )
    return gin[None], gout[None], total


def solution(mesh):
    placed = (
        P("dp", "fsdp", None, None, None),
        P("fsdp", "dp"),
        P("dp", "fsdp", None),
        P("fsdp", None),
        P("dp", "fsdp", None, None, None),
        P("fsdp", None),
        P(),
        P(),
        P("fsdp", None),
        P("fsdp", None),
    )
    return jax.shard_map(
        on_device,
        mesh=mesh,
        in_specs=placed,
        out_specs=(P("dp", "fsdp", None), P("dp", "fsdp", None), P()),
        check_vma=False,
    )
```

```python
import functools

import jax
import jax.numpy as jnp
from jax import lax
from jax.experimental import pallas as pl
from jax.experimental.pallas import tpu as pltpu
from jax.sharding import PartitionSpec as P

D = 1536
FF = 3072
K = 31
BR = 16
NB = 16
NH = 48
NDP = 64
ROWS = NB * BR
HALF = FF // 2
FSH = FF // 4
DSH = D // 4
SSH = 128
EPSILON = 1e-05
MESH = pl.DeviceIdType.MESH
F32 = jnp.float32
BF16 = jnp.bfloat16
VLIM = 62 * 1024 * 1024
LANES = 128

ANY = pl.BlockSpec(memory_space=pl.ANY)
VM = pl.BlockSpec(memory_space=pltpu.VMEM)
SM = pl.BlockSpec(memory_space=pltpu.SMEM)


def place():
    dp, f = lax.axis_index("dp"), lax.axis_index("fsdp")
    return dp, f, dp // 16, (dp // 8) % 2, dp % 8, f // 2, f % 2


def dev(x, yl, z, yh, c):
    return ((x * 2 + yl) * 8 + z, yh * 2 + c)


def greet(peers, extra=0):
    bar = pltpu.get_barrier_semaphore()
    for peer in peers:
        pl.semaphore_signal(bar, inc=1, device_id=peer, device_id_type=MESH)
    pl.semaphore_wait(bar, len(peers) + extra)


def remote(src, dst, send, recv, device):
    return pltpu.make_async_remote_copy(
        src_ref=src, dst_ref=dst, send_sem=send, recv_sem=recv, device_id=device, device_id_type=MESH
    )


class Sent:
    def __init__(self, src, dst, ss, rs, i, device):
        self.sems, self.device = (ss.at[i], rs.at[i]), device
        self.copy = remote(src, dst, *self.sems, device)

    def start(self):
        self.copy.start()

    def wait(self):
        self.copy.wait()

    def wait_send(self):
        self.copy.wait_send()

    def wait_got(self, ref):
        remote(ref, ref, *self.sems, self.device).wait_recv()


def nt(left, right):
    return lax.dot_general(left, right, (((1,), (1,)), ((), ())), preferred_element_type=F32)


def lane(start, size):
    return pl.ds(pl.multiple_of(start, LANES), size)


def rows(start, size):
    return pl.ds(pl.multiple_of(start, 16), size)


def kernel(
    count_in, rows_in, order_in, frames_hbm, taps, gain, cot, w_in, w_out, sub,
    gin, gout, ktot,
    frames, ginv, goutv, mine, invv, inv, slots, table, stab, ends, sbuf, rbuf, blocks, rowv, cots, masked, winv, woutv, suba, stage,
    hgr, nall, pgrad, hturn, nturn, picks, patch, maskv, texp, fch, feat, conv, mix, ngrad, part, got,
    tapp, sums, r1, s1, r2, s2, r3,
    ts, tr, as_, ar, ss, rs, ls, gs, gr, ps, pr, os_,
):
    dp, f, x, yl, z, yh, c = place()
    y = yh * 2 + yl
    fs, fo, fso = yh * 2 + 1 - c, (1 - yh) * 2 + c, (1 - yh) * 2 + 1 - c
    color = lax.rem(x + 2 * z, 4)
    across, mate = dev(x, 1 - yl, z, 1 - yh, c), dev(x, 1 - yl, z, yh, c)
    sibling, other, diagonal = (dp, fs), (dp, fo), (dp, fso)
    xp, xm = dev(lax.rem(x + 1, 4), yl, z, yh, c), dev(lax.rem(x + 3, 4), yl, z, yh, c)
    zp, zm = dev(x, yl, lax.rem(z + 1, 8), yh, c), dev(x, yl, lax.rem(z + 7, 8), yh, c)
    near, far = z * 2 + c, x * 4 + y

    def near_dev(i):
        return dev(x, yl, i // 2, yh, lax.rem(i, 2))

    def far_dev(i):
        return dev(i // 4, lax.rem(i, 2), z, lax.rem(i, 4) // 2, c)

    frames_in = pltpu.make_async_copy(frames_hbm, frames, ls.at[5])
    frames_in.start()
    mine[0] = jnp.full((1, LANES), count_in[0, 0], jnp.int32)
    mine[0, :, pl.ds(0, NH)] = rows_in[...]
    bar = pltpu.get_barrier_semaphore()

    def signal(k, carry):
        pl.semaphore_signal(bar, inc=1, device_id=(lax.rem(dp + k, NDP), f), device_id_type=MESH)
        return carry

    def signal_near(k, carry):
        zz, xy = lax.rem(z + k, 8), lax.rem(x * 2 + yl + k, 8)
        pl.semaphore_signal(bar, inc=1, device_id=dev(x, yl, zz, yh, 1 - c), device_id_type=MESH)
        pl.semaphore_signal(bar, inc=1, device_id=dev(xy // 2, lax.rem(xy, 2), z, 1 - yh, c), device_id_type=MESH)
        return carry

    lax.fori_loop(1, NDP, signal, 0)
    lax.fori_loop(1, 8, signal_near, 0)
    greet([sibling, other, diagonal], NDP - 1 + 14)

    count = iter(range(64))

    def rcopy(src, dst, device):
        return Sent(src, dst, ss, rs, next(count), device)

    def cols(g):
        return lane(g * FSH, FSH)

    lo, hi = pl.ds(0, FSH), pl.ds(FSH, FSH)

    table[0] = mine[0]

    def send_table(k, carry):
        remote(mine.at[pl.ds(0, 1)], table.at[pl.ds(k, 1)], ts, tr, (lax.rem(dp + k, NDP), f)).start()
        return carry

    lax.fori_loop(1, NDP, send_table, 0)
    home = lax.broadcasted_iota(jnp.int32, (NDP, NDP), 0)
    residue = lax.broadcasted_iota(jnp.int32, (NDP, NDP), 1)
    picked = jnp.where(order_in[...] == home, residue, 0)
    invv[...] = jnp.broadcast_to(jnp.sum(picked, axis=1, keepdims=True), (NDP, LANES))
    inv_copy = pltpu.make_async_copy(invv, inv, ls.at[6])
    inv_copy.start()

    def eighth(size):
        return color * 2 * size + yl * size

    q = rows(eighth(48), 48)
    qd = rows(f * DSH + eighth(48), 48)
    qx = rows(color * 96 + (1 - yl) * 48, 48)
    qxd = rows(f * DSH + color * 96 + (1 - yl) * 48, 48)
    sx = rows(color * 32 + (1 - yl) * 16, 16)
    sxd = rows(f * SSH + color * 32 + (1 - yl) * 16, 16)
    ox = rows(color * 192 + (1 - yl) * 96, 96)
    oxd = rows(FSH + color * 192 + (1 - yl) * 96, 96)
    y_sub = [rcopy(sub.at[sx], suba.at[sxd], across)]
    y_out = [rcopy(w_out.at[ox], woutv.at[oxd], across)]
    y_in = [
        rcopy(w_in.at[qx, cols(fo)], winv.at[qxd, lo], across),
        rcopy(w_in.at[qx, cols(f)], winv.at[qxd, hi], across),
        rcopy(w_in.at[qx, cols(fso)], stage.at[qx, lo], across),
        rcopy(w_in.at[qx, cols(fs)], stage.at[qx, hi], across),
    ]
    for copy in y_sub + y_out + y_in:
        copy.start()
    own = rows(f * DSH, DSH)
    on_chip = [
        rcopy(sub, suba.at[rows(f * SSH, SSH)], sibling),
        rcopy(cot, cots.at[1], sibling),
        rcopy(w_in.at[:, cols(fs)], winv.at[own, lo], sibling),
        rcopy(w_in.at[:, cols(fso)], winv.at[own, hi], sibling),
    ]
    local = [
        pltpu.make_async_copy(cot, cots.at[0], ls.at[0]),
        pltpu.make_async_copy(sub, suba.at[rows(f * SSH, SSH)], ls.at[1]),
        pltpu.make_async_copy(w_out, woutv.at[pl.ds(0, FSH)], ls.at[2]),
        pltpu.make_async_copy(w_in.at[:, cols(f)], winv.at[own, lo], ls.at[3]),
        pltpu.make_async_copy(w_in.at[:, cols(fo)], winv.at[own, hi], ls.at[4]),
    ]
    for copy in on_chip + local:
        copy.start()

    def settle(pairs):
        for copy, ref in pairs:
            copy.wait_send()
        for copy, ref in pairs:
            copy.wait_got(ref)

    def eighths(start, size, shift, part_of):
        return rows(start + lax.rem(color + shift, 4) * 2 * size + part_of * size, size)

    def pass_on(ref, start, size):
        here = ref.at[eighths(start, size, 0, yl)]
        copies = [rcopy(here, here, peer) for peer in (mate, xp, xm, zp)]
        for copy in copies:
            copy.start()
        spots = [(0, 1 - yl), (3, yl), (1, yl), (2, yl)]
        return [(copy, ref.at[eighths(start, size, *spot)]) for copy, spot in zip(copies, spots)]

    def pass_mate(ref, start, size, pairs):
        settle(pairs[:1])
        here = ref.at[eighths(start, size, 0, 1 - yl)]
        copies = [rcopy(here, here, peer) for peer in (xp, xm, zm)]
        for copy in copies:
            copy.start()
        spots = [(3, 1 - yl), (1, 1 - yl), (2, 1 - yl)]
        return pairs[1:] + [(copy, ref.at[eighths(start, size, *spot)]) for copy, spot in zip(copies, spots)]

    y_sub[0].wait_send()
    y_sub[0].wait_got(suba.at[rows(fo * SSH + eighth(16), 16)])
    all_sub = pass_on(suba, fo * SSH, 16)

    rest = table.at[pl.ds(1, NDP - 1)]
    remote(rest, rest, ts, tr, other).wait()
    to_scalar = pltpu.make_async_copy(table, stab, ls.at[7])
    to_scalar.start()
    to_scalar.wait()
    inv_copy.wait()
    frames_in.wait()

    def running(i, total):
        total = total + stab[lax.rem(dp - i + NDP, NDP), 0, NH]
        ends[i] = total
        return total

    lax.fori_loop(0, NDP, running, 0)
    start = ends[dp] - stab[0, 0, NH]

    def pick_home(j):
        return frames[jnp.minimum(lax.rem(inv[j, 0] - start + NDP * NH, NDP), NH - 1)]

    def send(k, carry):
        kk = lax.rem(k * 27, NDP)
        to = lax.rem(dp + kk, NDP)
        sbuf[to] = pick_home(to)
        remote(sbuf.at[to], rbuf.at[kk], as_, ar, (to, f)).start()
        return carry

    lax.fori_loop(1, NDP, send, 0)
    rbuf[0] = pick_home(dp)

    y_out[0].wait_send()
    y_out[0].wait_got(woutv.at[rows(FSH + eighth(96), 96)])
    all_out = pass_on(woutv, FSH, 96)
    all_sub = pass_mate(suba, fo * SSH, 16, all_sub)
    for copy in y_in:
        copy.wait_send()
    qi = rows(fo * DSH + eighth(48), 48)
    for copy, ref in zip(y_in, [winv.at[qi, lo], winv.at[qi, hi], stage.at[q, lo], stage.at[q, hi]]):
        copy.wait_got(ref)
    all_stage = pass_on(stage, 0, 48)
    all_in_w = pass_on(winv, fo * DSH, 48)
    all_out = pass_mate(woutv, FSH, 96, all_out)
    all_stage = pass_mate(stage, 0, 48, all_stage)
    all_in_w = pass_mate(winv, fo * DSH, 48, all_in_w)

    first = inv[dp, 0]

    def choose(m, height):
        wanted = first + NDP * m
        at = 0
        for step in (32, 16, 8, 4, 2, 1):
            at = jnp.where(ends[at + step - 1] <= wanted, at + step, at)
        slot = lax.rem(dp - at + NDP, NDP)
        within = jnp.clip(wanted - (ends[at] - stab[slot, 0, NH]), 0, NH - 1)
        slots[m] = slot
        spot = lax.broadcasted_iota(jnp.int32, (NB, LANES), 0)
        return jnp.where(spot == m, stab[slot, 0, within], height)

    rowv[0] = lax.fori_loop(0, NB, choose, jnp.zeros((NB, LANES), jnp.int32))

    r = lax.broadcasted_iota(jnp.int32, (ROWS, 4 * ROWS), 0)
    col = lax.broadcasted_iota(jnp.int32, (ROWS, 4 * ROWS), 1)
    want = lax.rem(r, NB) * (4 * BR) + 4 * (r // NB)
    for k in range(4):
        picks[k] = jnp.where(col == want + k, 1.0, 0.0).astype(BF16)

    def turned(g):
        r = lax.broadcasted_iota(jnp.int32, (ROWS, ROWS), 0)
        col = lax.broadcasted_iota(jnp.int32, (ROWS, ROWS), 1)
        turn = jnp.where(col == lax.rem(r, NB) * BR + r // NB, 1.0, 0.0).astype(BF16)
        return jnp.dot(turn, cots[g], preferred_element_type=F32).astype(BF16)

    def hidden_grads(p):
        span = pl.ds(p * 2 * ROWS, 2 * ROWS)

        def tile(n, carry):
            w = lane(n * 256, 256)
            hgr[span, w] = 0.5 * nt(masked[span, :], woutv[w, :])
            return carry

        lax.fori_loop(0, HALF // 256, tile, 0)

    local[0].wait()
    masked[pl.ds(0, ROWS), :] = turned(0)
    on_chip[1].wait()
    masked[pl.ds(ROWS, ROWS), :] = turned(1)

    settle(all_sub)
    theirs = suba.at[rows(fo * SSH, SSH)]
    sub_sib = rcopy(theirs, theirs, sibling)
    sub_sib.start()

    every = rbuf.at[pl.ds(1, NDP - 1)]
    remote(every, every, as_, ar, other).wait()

    def select(m, carry):
        blocks[m] = rbuf[slots[m]]
        return carry

    lax.fori_loop(0, NB, select, 0)
    here = [
        rcopy(rowv.at[0], rowv.at[1], sibling),
        rcopy(rowv.at[0], rowv.at[2], other),
        rcopy(rowv.at[0], rowv.at[3], diagonal),
        rcopy(blocks.at[pl.ds(0, NB)], blocks.at[pl.ds(NB, NB)], other),
    ]
    for copy in here:
        copy.start()
    cot_other = rcopy(cot, cots.at[2], other)
    cot_other.start()
    local[1].wait()
    on_chip[0].wait_send()
    on_chip[0].wait_got(suba.at[rows(fs * SSH, SSH)])
    sub_sib.wait_send()
    sub_sib.wait_got(suba.at[rows(fso * SSH, SSH)])

    def fill_mask(g):
        for t in range(BR):
            maskv[g, pl.ds(t * NB, NB), :] = jnp.where(rowv[g] > t, 1.0, 0.0)

    def front(b, g, row):
        fill_mask(g)
        x_in = blocks[pl.ds(b * NB, NB)].reshape(4 * ROWS, LANES)
        for k in range(4):
            patch[:, pl.ds(k * LANES, LANES)] = jnp.dot(picks[k], x_in, preferred_element_type=F32).astype(BF16)

        def project(n, carry):
            w = lane(n * 256, 256)
            total = jnp.dot(patch[...], suba[:, w], preferred_element_type=F32)
            feat[b, :, w] = (total * maskv[g, :, pl.ds(0, 1)]).astype(BF16)
            return carry

        lax.fori_loop(0, D // 256, project, 0)

        def chunk(l, carry):
            w = lane(l * LANES, LANES)
            for k in range(K):
                texp[pl.ds((K - 1 - k) * NB, NB), :] = jnp.broadcast_to(taps[pl.ds(k, 1), w], (NB, LANES))
            fch[...] = feat[b, :, w].astype(F32)
            total = jnp.zeros((BR, NB, LANES), F32)
            for s in range(BR):
                weights = texp[pl.ds((15 - s) * NB, ROWS), :].reshape(BR, NB, LANES)
                total += weights * fch[pl.ds(s * NB, NB), :][None]
            total = total.reshape(ROWS, LANES)
            if b == 0:
                conv[:, w] = total
            mix[:, w] = fch[...] + maskv[g] * (total * jax.nn.sigmoid(total))
            return carry

        lax.fori_loop(0, D // LANES, chunk, 0)

        def norm(i, carry):
            mixed = mix[rows(i * 64, 64), :]
            mean = jnp.mean(mixed, axis=-1, keepdims=True)
            centred = mixed - mean
            variance = jnp.mean(centred * centred, axis=-1, keepdims=True)
            nall[rows(row + i * 64, 64), :] = (centred * lax.rsqrt(variance + EPSILON) * gain[...][None, :]).astype(BF16)
            swap = nall.at[rows(row + i * 64, 64)], nall.at[rows(row + ROWS + i * 64, 64)]
            remote(*swap, ps.at[b * 4 + i], pr.at[b * 4 + i], sibling).start()
            return carry

        lax.fori_loop(0, ROWS // 64, norm, 0)

    def norm_here(b, row):
        def step(i, carry):
            swap = nall.at[rows(row + i * 64, 64)], nall.at[rows(row + ROWS + i * 64, 64)]
            remote(*swap, ps.at[b * 4 + i], pr.at[b * 4 + i], sibling).wait()
            return carry

        lax.fori_loop(0, ROWS // 64, step, 0)

    front(0, 0, 0)
    settle(all_stage)
    stage_sib = rcopy(stage, winv.at[rows(fo * DSH, DSH)], sibling)
    stage_sib.start()
    settle(all_out)
    local[2].wait()
    hidden_grads(0)

    def group(p):
        span = pl.ds(p * 2 * ROWS, 2 * ROWS)

        def tile(n, with_hidden):
            w = lane(n * 256, 256)
            pre = jnp.dot(nall[span, :], winv[:, w], preferred_element_type=F32)
            sig = jax.nn.sigmoid(pre)
            if with_hidden:
                hturn[rows(n * 256, 256), span] = (pre * sig).astype(BF16).T
            mask = jnp.concatenate([maskv[2 * p], maskv[2 * p + 1]], axis=0)[:, :1]
            pgrad[span, w] = (mask * hgr[span, w] * (sig * (1.0 + pre * (1.0 - sig)))).astype(BF16)

        def both(n, carry):
            tile(n, True)
            tile(n + 3, False)
            return carry

        lax.fori_loop(0, HALF // 512, both, 0)

    def turn_normed(p):
        span = pl.ds(p * 2 * ROWS, 2 * ROWS)
        for i, which in enumerate((fs, f)):
            nturn[pl.ds(i * DSH, DSH), span] = nall[span, lane(which * DSH, DSH)].T

    def given(n):
        w = lane(n * 256, 256)
        return remote(part.at[:, w], got.at[:, w], ps.at[8 + n], pr.at[8 + n], sibling)

    def back(g, ref):
        def tile(n, carry):
            w = lane(n * 256, 256)
            ref[:, w] = nt(pgrad[pl.ds(g * ROWS, ROWS), :], winv[w, :])
            if g == 1:
                given(n).start()
            return carry

        lax.fori_loop(0, D // 256, tile, 0)

    here[0].wait()
    fill_mask(1)
    norm_here(0, 0)
    turn_normed(0)
    settle(all_in_w)
    local[3].wait()
    local[4].wait()
    for i, half in ((2, lo), (3, hi)):
        on_chip[i].wait_send()
        on_chip[i].wait_got(winv.at[rows(fs * DSH, DSH), half])
    stage_sib.wait_send()
    stage_sib.wait_got(winv.at[rows(fso * DSH, DSH)])
    group(0)
    back(1, part)
    back(0, ngrad)

    def take(n, carry):
        given(n).wait()
        return carry

    lax.fori_loop(0, D // 256, take, 0)

    def norm_back(i, carry):
        span = rows(i * 64, 64)
        mask = maskv[0, span, :][:, :1]
        pre = conv[span, :]
        sig = jax.nn.sigmoid(pre)
        mixed = feat[0, span, :].astype(F32) + mask * (pre * sig)
        mean = jnp.mean(mixed, axis=-1, keepdims=True)
        centred = mixed - mean
        scale = lax.rsqrt(jnp.mean(centred * centred, axis=-1, keepdims=True) + EPSILON)
        hat = centred * scale
        dn = (ngrad[span, :] + got[span, :]) * gain[...][None, :]
        m1 = jnp.mean(dn, axis=-1, keepdims=True)
        m2 = jnp.mean(dn * hat, axis=-1, keepdims=True)
        total = mask * masked[span, :].astype(F32) + scale * (dn - m1 - hat * m2)
        mix[span, :] = mask * total * (sig * (1.0 + pre * (1.0 - sig)))
        return carry

    lax.fori_loop(0, ROWS // 64, norm_back, 0)

    def tap_chunk(l, carry):
        w = lane(l * LANES, LANES)
        fch[...] = feat[0, :, w].astype(F32)
        for k in range(K):
            t0, t1 = max(0, 15 - k), min(BR, 31 - k)
            size = (t1 - t0) * NB
            term = mix[pl.ds(t0 * NB, size), w] * fch[pl.ds((t0 + k - 15) * NB, size), :]
            sums[pl.ds(k, 1), :] = jnp.sum(term, axis=0, keepdims=True)
        sums[pl.ds(K, 1), :] = jnp.zeros((1, LANES), F32)
        tapp[pl.ds(pl.multiple_of(l * (K + 1), 8), K + 1), :] = sums[...]
        return carry

    lax.fori_loop(0, D // LANES, tap_chunk, 0)

    def spread(make):
        def step(k, carry):
            make(k).start()
            return carry

        lax.fori_loop(1, 16, step, 0)

    def rows24(i):
        return pl.ds(pl.multiple_of(i * 24, 8), 24)

    def one(k):
        to = lax.rem(near + k, 16)
        return remote(tapp.at[rows24(to)], r1.at[k], gs.at[0], gr.at[0], near_dev(to))

    def two(k):
        to = lax.rem(far + k, 16)
        return remote(s1, r2.at[k], gs.at[1], gr.at[1], far_dev(to))

    def three(k):
        to = lax.rem(near + k, 16)
        return remote(s2, r3.at[k], gs.at[2], gr.at[2], near_dev(to))

    def all_here(ref, stage_no):
        every = ref.at[pl.ds(1, 15)]
        remote(every, every, gs.at[stage_no], gr.at[stage_no], sibling).wait()

    def ordered(ref, mine_at):
        def step(i, total):
            return total + ref[lax.rem(mine_at - i + 16, 16)]

        return lax.fori_loop(0, 16, step, jnp.zeros((24, LANES), F32))

    spread(one)
    here[1].wait()
    here[3].wait()
    front(1, 2, 2 * ROWS)
    here[2].wait()
    fill_mask(3)
    r1[0] = tapp[rows24(near), :]
    all_here(r1, 0)
    s1[...] = ordered(r1, near)
    spread(two)
    cot_other.wait()
    cot_sib = rcopy(cots.at[2], cots.at[3], sibling)
    cot_sib.start()
    masked[pl.ds(2 * ROWS, ROWS), :] = turned(2)
    cot_sib.wait()
    masked[pl.ds(3 * ROWS, ROWS), :] = turned(3)
    hidden_grads(1)
    for g in range(4):
        if g == 2:
            norm_here(1, 2 * ROWS)
            turn_normed(1)
            group(1)
        span = pl.ds(g * ROWS, ROWS)
        masked[span, :] = jnp.where(maskv[g][:, :1] > 0, masked[span, :].astype(F32), 0.0).astype(BF16)
    r2[0] = s1[...]
    all_here(r2, 1)
    s2[...] = ordered(r2, far)
    spread(three)

    def gin_tile(i, n):
        return jnp.dot(
            nturn[pl.ds(i * DSH, DSH), :], pgrad[:, lane(n * 256, 256)], preferred_element_type=F32
        ).astype(BF16)

    def give_tile(n, carry):
        stage[:, lane(n * 256, 256)] = gin_tile(0, n)
        return carry

    lax.fori_loop(0, 6, give_tile, 0)
    swaps = [rcopy(stage.at[:, half], ginv.at[:, cols(g)], sibling) for half, g in ((lo, f), (hi, fo))]
    for swap in swaps:
        swap.start()

    def leave(ref, out, w, i):
        return pltpu.make_async_copy(ref.at[:, w], out.at[:, w], os_.at[i])

    def keep_tile(n, carry):
        first, second = lane(f * FSH + n * 256, 256), lane(fo * FSH + n * 256, 256)
        ginv[:, first] = gin_tile(1, n)
        leave(ginv, gin, first, n).start()
        ginv[:, second] = gin_tile(1, n + 3)
        leave(ginv, gin, second, 3 + n).start()
        return carry

    lax.fori_loop(0, 3, keep_tile, 0)

    def gout_tile(n, carry):
        w = lane(n * 256, 256)
        goutv[:, w] = (0.5 * jnp.dot(hturn[...], masked[:, w], preferred_element_type=F32)).astype(BF16)
        leave(goutv, gout, w, 6 + n).start()
        return carry

    lax.fori_loop(0, D // 256, gout_tile, 0)
    for i, (swap, g) in enumerate(zip(swaps, (fs, fso))):
        swap.wait_send()
        swap.wait_got(ginv.at[:, cols(g)])
        leave(ginv, gin, cols(g), 12 + i).start()
    r3[0] = s2[...]
    all_here(r3, 2)

    def lay(k, carry):
        tapp[rows24(lax.rem(near - k + 16, 16)), :] = r3[k] * (1.0 / ROWS)
        return carry

    lax.fori_loop(0, 16, lay, 0)
    for l in range(D // LANES):
        ktot[:, pl.ds(l * LANES, LANES)] = tapp[pl.ds(l * (K + 1), K), :]

    def gone(n, carry):
        leave(ginv, gin, lane(f * FSH + n * 256, 256), n).wait()
        leave(ginv, gin, lane(fo * FSH + n * 256, 256), 3 + n).wait()
        leave(goutv, gout, lane(n * 256, 256), 6 + n).wait()
        leave(goutv, gout, lane((n + 3) * 256, 256), 9 + n).wait()
        return carry

    lax.fori_loop(0, 3, gone, 0)
    for i, g in enumerate((fs, fso)):
        leave(ginv, gin, cols(g), 12 + i).wait()


def on_device(
    frames, occupied_slot_counts, block_frame_rows, order, cotangent, sub_weight, depth_kernel, norm_gain, w_in, w_out
):
    vm, dma = pltpu.VMEM, pltpu.SemaphoreType.DMA
    stages, one = vm((16, 24, LANES), F32), vm((24, LANES), F32)
    gin, gout, total = pl.pallas_call(
        kernel,
        out_shape=[
            jax.ShapeDtypeStruct((DSH, FF), BF16),
            jax.ShapeDtypeStruct((FSH, D), BF16),
            jax.ShapeDtypeStruct((K, D), F32),
        ],
        in_specs=[SM, VM, VM, ANY, VM, VM, ANY, ANY, ANY, ANY],
        out_specs=[ANY, ANY, VM],
        scratch_shapes=[
            vm((NH, 64, LANES), BF16),
            vm((DSH, FF), BF16),
            vm((FSH, D), BF16),
            vm((1, 1, LANES), jnp.int32),
            vm((NDP, LANES), jnp.int32),
            pltpu.SMEM((NDP, LANES), jnp.int32),
            pltpu.SMEM((NB,), jnp.int32),
            vm((NDP, 1, LANES), jnp.int32),
            pltpu.SMEM((NDP, 1, LANES), jnp.int32),
            pltpu.SMEM((NDP,), jnp.int32),
            vm((NDP, 64, LANES), BF16),
            vm((NDP, 64, LANES), BF16),
            vm((2 * NB, 64, LANES), BF16),
            vm((4, NB, LANES), jnp.int32),
            vm((4, ROWS, D), BF16),
            vm((4 * ROWS, D), BF16),
            vm((D, HALF), BF16),
            vm((HALF, D), BF16),
            vm((4 * SSH, D), BF16),
            vm((DSH, HALF), BF16),
            vm((4 * ROWS, HALF), F32),
            vm((4 * ROWS, D), BF16),
            vm((4 * ROWS, HALF), BF16),
            vm((FSH, 4 * ROWS), BF16),
            vm((2 * DSH, 4 * ROWS), BF16),
            vm((4, ROWS, 4 * ROWS), BF16),
            vm((ROWS, 4 * LANES), BF16),
            vm((4, ROWS, LANES), F32),
            vm((K * NB, LANES), F32),
            vm((ROWS, LANES), F32),
            vm((2, ROWS, D), BF16),
            vm((ROWS, D), F32),
            vm((ROWS, D), F32),
            vm((ROWS, D), F32),
            vm((ROWS, D), F32),
            vm((ROWS, D), F32),
            vm((D // LANES * (K + 1), LANES), F32),
            vm((K + 1, LANES), F32),
            stages, one, stages, one, stages,
            dma, dma, dma, dma,
            dma((56,)), dma((56,)), dma((8,)), dma((3,)), dma((3,)), dma((14,)), dma((14,)), dma((14,)),
        ],
        compiler_params=pltpu.CompilerParams(collective_id=1, has_side_effects=True, vmem_limit_bytes=VLIM),
        name="window",
    )(
        occupied_slot_counts, block_frame_rows[0], order, frames[0, 0], depth_kernel, norm_gain,
        cotangent[0, 0].reshape(ROWS, D), w_in, w_out, sub_weight,
    )
    return gin[None], gout[None], total


def solution(mesh):
    placed = (
        P("dp", "fsdp", None, None, None),
        P("fsdp", "dp"),
        P("dp", "fsdp", None),
        P("fsdp", None),
        P("dp", "fsdp", None, None, None),
        P("fsdp", None),
        P(),
        P(),
        P("fsdp", None),
        P("fsdp", None),
    )
    return jax.shard_map(
        on_device,
        mesh=mesh,
        in_specs=placed,
        out_specs=(P("dp", "fsdp", None), P("dp", "fsdp", None), P()),
        check_vma=False,
    )
```

```python
import functools

import jax
import jax.numpy as jnp
from jax import lax
from jax.experimental import pallas as pl
from jax.experimental.pallas import tpu as pltpu
from jax.sharding import PartitionSpec as P

D = 1536
FF = 3072
K = 31
BR = 16
NB = 16
NH = 48
NDP = 64
ROWS = NB * BR
HALF = FF // 2
FSH = FF // 4
DSH = D // 4
SSH = 128
EPSILON = 1e-05
MESH = pl.DeviceIdType.MESH
F32 = jnp.float32
BF16 = jnp.bfloat16
VLIM = 62 * 1024 * 1024
LANES = 128

ANY = pl.BlockSpec(memory_space=pl.ANY)
VM = pl.BlockSpec(memory_space=pltpu.VMEM)
SM = pl.BlockSpec(memory_space=pltpu.SMEM)


def place():
    dp, f = lax.axis_index("dp"), lax.axis_index("fsdp")
    return dp, f, dp // 16, (dp // 8) % 2, dp % 8, f // 2, f % 2


def dev(x, yl, z, yh, c):
    return ((x * 2 + yl) * 8 + z, yh * 2 + c)


def greet(peers, extra=0):
    bar = pltpu.get_barrier_semaphore()
    for peer in peers:
        pl.semaphore_signal(bar, inc=1, device_id=peer, device_id_type=MESH)
    pl.semaphore_wait(bar, len(peers) + extra)


def remote(src, dst, send, recv, device):
    return pltpu.make_async_remote_copy(
        src_ref=src, dst_ref=dst, send_sem=send, recv_sem=recv, device_id=device, device_id_type=MESH
    )


class Sent:
    def __init__(self, src, dst, ss, rs, i, device):
        self.sems, self.device = (ss.at[i], rs.at[i]), device
        self.copy = remote(src, dst, *self.sems, device)

    def start(self):
        self.copy.start()

    def wait(self):
        self.copy.wait()

    def wait_send(self):
        self.copy.wait_send()

    def wait_got(self, ref):
        remote(ref, ref, *self.sems, self.device).wait_recv()


def nt(left, right):
    return lax.dot_general(left, right, (((1,), (1,)), ((), ())), preferred_element_type=F32)


def lane(start, size):
    return pl.ds(pl.multiple_of(start, LANES), size)


def rows(start, size):
    return pl.ds(pl.multiple_of(start, 16), size)


def kernel(
    count_in, rows_in, order_in, frames_hbm, taps, gain, cot, w_in, w_out, sub,
    gin, gout, ktot,
    frames, ginv, goutv, mine, invv, inv, slots, table, stab, ends, sbuf, rbuf, blocks, rowv, cots, masked, winv, woutv, suba, stage,
    hgr, nall, pgrad, hturn, nturn, picks, patch, maskv, texp, fch, feat, conv, mix, ngrad, part, got,
    tapp, sums, r1, s1, r2, s2, r3,
    ts, tr, as_, ar, ss, rs, ls, gs, gr, ps, pr, os_,
):
    dp, f, x, yl, z, yh, c = place()
    y = yh * 2 + yl
    fs, fo, fso = yh * 2 + 1 - c, (1 - yh) * 2 + c, (1 - yh) * 2 + 1 - c
    color = lax.rem(x + 2 * z, 4)
    across, mate = dev(x, 1 - yl, z, 1 - yh, c), dev(x, 1 - yl, z, yh, c)
    sibling, other, diagonal = (dp, fs), (dp, fo), (dp, fso)
    xp, xm = dev(lax.rem(x + 1, 4), yl, z, yh, c), dev(lax.rem(x + 3, 4), yl, z, yh, c)
    zp, zm = dev(x, yl, lax.rem(z + 1, 8), yh, c), dev(x, yl, lax.rem(z + 7, 8), yh, c)
    near, far = z * 2 + c, x * 4 + y

    def near_dev(i):
        return dev(x, yl, i // 2, yh, lax.rem(i, 2))

    def far_dev(i):
        return dev(i // 4, lax.rem(i, 2), z, lax.rem(i, 4) // 2, c)

    frames_in = pltpu.make_async_copy(frames_hbm, frames, ls.at[5])
    frames_in.start()
    mine[0] = jnp.full((1, LANES), count_in[0, 0], jnp.int32)
    mine[0, :, pl.ds(0, NH)] = rows_in[...]
    bar = pltpu.get_barrier_semaphore()

    def signal(k, carry):
        pl.semaphore_signal(bar, inc=1, device_id=(lax.rem(dp + k, NDP), f), device_id_type=MESH)
        return carry

    def signal_near(k, carry):
        zz, xy = lax.rem(z + k, 8), lax.rem(x * 2 + yl + k, 8)
        pl.semaphore_signal(bar, inc=1, device_id=dev(x, yl, zz, yh, 1 - c), device_id_type=MESH)
        pl.semaphore_signal(bar, inc=1, device_id=dev(xy // 2, lax.rem(xy, 2), z, 1 - yh, c), device_id_type=MESH)
        return carry

    lax.fori_loop(1, NDP, signal, 0)
    lax.fori_loop(1, 8, signal_near, 0)
    greet([sibling, other, diagonal], NDP - 1 + 14)

    count = iter(range(64))

    def rcopy(src, dst, device):
        return Sent(src, dst, ss, rs, next(count), device)

    def cols(g):
        return lane(g * FSH, FSH)

    lo, hi = pl.ds(0, FSH), pl.ds(FSH, FSH)

    table[0] = mine[0]

    def send_table(k, carry):
        remote(mine.at[pl.ds(0, 1)], table.at[pl.ds(k, 1)], ts, tr, (lax.rem(dp + k, NDP), f)).start()
        return carry

    lax.fori_loop(1, NDP, send_table, 0)
    home = lax.broadcasted_iota(jnp.int32, (NDP, NDP), 0)
    residue = lax.broadcasted_iota(jnp.int32, (NDP, NDP), 1)
    picked = jnp.where(order_in[...] == home, residue, 0)
    invv[...] = jnp.broadcast_to(jnp.sum(picked, axis=1, keepdims=True), (NDP, LANES))
    inv_copy = pltpu.make_async_copy(invv, inv, ls.at[6])
    inv_copy.start()

    def eighth(size):
        return color * 2 * size + yl * size

    q = rows(eighth(48), 48)
    qd = rows(f * DSH + eighth(48), 48)
    qx = rows(color * 96 + (1 - yl) * 48, 48)
    qxd = rows(f * DSH + color * 96 + (1 - yl) * 48, 48)
    sx = rows(color * 32 + (1 - yl) * 16, 16)
    sxd = rows(f * SSH + color * 32 + (1 - yl) * 16, 16)
    ox = rows(color * 192 + (1 - yl) * 96, 96)
    oxd = rows(FSH + color * 192 + (1 - yl) * 96, 96)
    y_sub = [rcopy(sub.at[sx], suba.at[sxd], across)]
    y_out = [rcopy(w_out.at[ox], woutv.at[oxd], across)]
    y_in = [
        rcopy(w_in.at[qx, cols(fo)], winv.at[qxd, lo], across),
        rcopy(w_in.at[qx, cols(f)], winv.at[qxd, hi], across),
        rcopy(w_in.at[qx, cols(fso)], stage.at[qx, lo], across),
        rcopy(w_in.at[qx, cols(fs)], stage.at[qx, hi], across),
    ]
    for copy in y_sub + y_out + y_in:
        copy.start()
    own = rows(f * DSH, DSH)
    on_chip = [
        rcopy(sub, suba.at[rows(f * SSH, SSH)], sibling),
        rcopy(cot, cots.at[1], sibling),
        rcopy(w_in.at[:, cols(fs)], winv.at[own, lo], sibling),
        rcopy(w_in.at[:, cols(fso)], winv.at[own, hi], sibling),
    ]
    local = [
        pltpu.make_async_copy(cot, cots.at[0], ls.at[0]),
        pltpu.make_async_copy(sub, suba.at[rows(f * SSH, SSH)], ls.at[1]),
        pltpu.make_async_copy(w_out, woutv.at[pl.ds(0, FSH)], ls.at[2]),
        pltpu.make_async_copy(w_in.at[:, cols(f)], winv.at[own, lo], ls.at[3]),
        pltpu.make_async_copy(w_in.at[:, cols(fo)], winv.at[own, hi], ls.at[4]),
    ]
    for copy in on_chip + local:
        copy.start()

    def settle(pairs):
        for copy, ref in pairs:
            copy.wait_send()
        for copy, ref in pairs:
            copy.wait_got(ref)

    def eighths(start, size, shift, part_of):
        return rows(start + lax.rem(color + shift, 4) * 2 * size + part_of * size, size)

    def pass_on(ref, start, size):
        here = ref.at[eighths(start, size, 0, yl)]
        copies = [rcopy(here, here, peer) for peer in (mate, xp, xm, zp)]
        for copy in copies:
            copy.start()
        spots = [(0, 1 - yl), (3, yl), (1, yl), (2, yl)]
        return [(copy, ref.at[eighths(start, size, *spot)]) for copy, spot in zip(copies, spots)]

    def pass_mate(ref, start, size, pairs):
        settle(pairs[:1])
        here = ref.at[eighths(start, size, 0, 1 - yl)]
        copies = [rcopy(here, here, peer) for peer in (xp, xm, zm)]
        for copy in copies:
            copy.start()
        spots = [(3, 1 - yl), (1, 1 - yl), (2, 1 - yl)]
        return pairs[1:] + [(copy, ref.at[eighths(start, size, *spot)]) for copy, spot in zip(copies, spots)]

    y_sub[0].wait_send()
    y_sub[0].wait_got(suba.at[rows(fo * SSH + eighth(16), 16)])
    all_sub = pass_on(suba, fo * SSH, 16)

    rest = table.at[pl.ds(1, NDP - 1)]
    remote(rest, rest, ts, tr, other).wait()
    to_scalar = pltpu.make_async_copy(table, stab, ls.at[7])
    to_scalar.start()
    to_scalar.wait()
    inv_copy.wait()
    frames_in.wait()

    def running(i, total):
        total = total + stab[lax.rem(dp - i + NDP, NDP), 0, NH]
        ends[i] = total
        return total

    lax.fori_loop(0, NDP, running, 0)
    start = ends[dp] - stab[0, 0, NH]

    def pick_home(j):
        return frames[jnp.minimum(lax.rem(inv[j, 0] - start + NDP * NH, NDP), NH - 1)]

    def send(k, carry):
        kk = lax.rem(k * 37, NDP)
        to = lax.rem(dp + kk, NDP)
        sbuf[to] = pick_home(to)
        remote(sbuf.at[to], rbuf.at[kk], as_, ar, (to, f)).start()
        return carry

    lax.fori_loop(1, NDP, send, 0)
    rbuf[0] = pick_home(dp)

    y_out[0].wait_send()
    y_out[0].wait_got(woutv.at[rows(FSH + eighth(96), 96)])
    all_out = pass_on(woutv, FSH, 96)
    all_sub = pass_mate(suba, fo * SSH, 16, all_sub)
    for copy in y_in:
        copy.wait_send()
    qi = rows(fo * DSH + eighth(48), 48)
    for copy, ref in zip(y_in, [winv.at[qi, lo], winv.at[qi, hi], stage.at[q, lo], stage.at[q, hi]]):
        copy.wait_got(ref)
    all_stage = pass_on(stage, 0, 48)
    all_in_w = pass_on(winv, fo * DSH, 48)
    all_out = pass_mate(woutv, FSH, 96, all_out)
    all_stage = pass_mate(stage, 0, 48, all_stage)
    all_in_w = pass_mate(winv, fo * DSH, 48, all_in_w)

    first = inv[dp, 0]

    def choose(m, height):
        wanted = first + NDP * m
        at = 0
        for step in (32, 16, 8, 4, 2, 1):
            at = jnp.where(ends[at + step - 1] <= wanted, at + step, at)
        slot = lax.rem(dp - at + NDP, NDP)
        within = jnp.clip(wanted - (ends[at] - stab[slot, 0, NH]), 0, NH - 1)
        slots[m] = slot
        spot = lax.broadcasted_iota(jnp.int32, (NB, LANES), 0)
        return jnp.where(spot == m, stab[slot, 0, within], height)

    rowv[0] = lax.fori_loop(0, NB, choose, jnp.zeros((NB, LANES), jnp.int32))

    r = lax.broadcasted_iota(jnp.int32, (ROWS, 4 * ROWS), 0)
    col = lax.broadcasted_iota(jnp.int32, (ROWS, 4 * ROWS), 1)
    want = lax.rem(r, NB) * (4 * BR) + 4 * (r // NB)
    for k in range(4):
        picks[k] = jnp.where(col == want + k, 1.0, 0.0).astype(BF16)

    def turned(g):
        r = lax.broadcasted_iota(jnp.int32, (ROWS, ROWS), 0)
        col = lax.broadcasted_iota(jnp.int32, (ROWS, ROWS), 1)
        turn = jnp.where(col == lax.rem(r, NB) * BR + r // NB, 1.0, 0.0).astype(BF16)
        return jnp.dot(turn, cots[g], preferred_element_type=F32).astype(BF16)

    def hidden_grads(p):
        span = pl.ds(p * 2 * ROWS, 2 * ROWS)

        def tile(n, carry):
            w = lane(n * 256, 256)
            hgr[span, w] = 0.5 * nt(masked[span, :], woutv[w, :])
            return carry

        lax.fori_loop(0, HALF // 256, tile, 0)

    local[0].wait()
    masked[pl.ds(0, ROWS), :] = turned(0)
    on_chip[1].wait()
    masked[pl.ds(ROWS, ROWS), :] = turned(1)

    settle(all_sub)
    theirs = suba.at[rows(fo * SSH, SSH)]
    sub_sib = rcopy(theirs, theirs, sibling)
    sub_sib.start()

    every = rbuf.at[pl.ds(1, NDP - 1)]
    remote(every, every, as_, ar, other).wait()

    def select(m, carry):
        blocks[m] = rbuf[slots[m]]
        return carry

    lax.fori_loop(0, NB, select, 0)
    here = [
        rcopy(rowv.at[0], rowv.at[1], sibling),
        rcopy(rowv.at[0], rowv.at[2], other),
        rcopy(rowv.at[0], rowv.at[3], diagonal),
        rcopy(blocks.at[pl.ds(0, NB)], blocks.at[pl.ds(NB, NB)], other),
    ]
    for copy in here:
        copy.start()
    cot_other = rcopy(cot, cots.at[2], other)
    cot_other.start()
    local[1].wait()
    on_chip[0].wait_send()
    on_chip[0].wait_got(suba.at[rows(fs * SSH, SSH)])
    sub_sib.wait_send()
    sub_sib.wait_got(suba.at[rows(fso * SSH, SSH)])

    def fill_mask(g):
        for t in range(BR):
            maskv[g, pl.ds(t * NB, NB), :] = jnp.where(rowv[g] > t, 1.0, 0.0)

    def front(b, g, row):
        fill_mask(g)
        x_in = blocks[pl.ds(b * NB, NB)].reshape(4 * ROWS, LANES)
        for k in range(4):
            patch[:, pl.ds(k * LANES, LANES)] = jnp.dot(picks[k], x_in, preferred_element_type=F32).astype(BF16)

        def project(n, carry):
            w = lane(n * 256, 256)
            total = jnp.dot(patch[...], suba[:, w], preferred_element_type=F32)
            feat[b, :, w] = (total * maskv[g, :, pl.ds(0, 1)]).astype(BF16)
            return carry

        lax.fori_loop(0, D // 256, project, 0)

        def chunk(l, carry):
            w = lane(l * LANES, LANES)
            for k in range(K):
                texp[pl.ds((K - 1 - k) * NB, NB), :] = jnp.broadcast_to(taps[pl.ds(k, 1), w], (NB, LANES))
            fch[...] = feat[b, :, w].astype(F32)
            total = jnp.zeros((BR, NB, LANES), F32)
            for s in range(BR):
                weights = texp[pl.ds((15 - s) * NB, ROWS), :].reshape(BR, NB, LANES)
                total += weights * fch[pl.ds(s * NB, NB), :][None]
            total = total.reshape(ROWS, LANES)
            if b == 0:
                conv[:, w] = total
            mix[:, w] = fch[...] + maskv[g] * (total * jax.nn.sigmoid(total))
            return carry

        lax.fori_loop(0, D // LANES, chunk, 0)

        def norm(i, carry):
            mixed = mix[rows(i * 64, 64), :]
            mean = jnp.mean(mixed, axis=-1, keepdims=True)
            centred = mixed - mean
            variance = jnp.mean(centred * centred, axis=-1, keepdims=True)
            nall[rows(row + i * 64, 64), :] = (centred * lax.rsqrt(variance + EPSILON) * gain[...][None, :]).astype(BF16)
            swap = nall.at[rows(row + i * 64, 64)], nall.at[rows(row + ROWS + i * 64, 64)]
            remote(*swap, ps.at[b * 4 + i], pr.at[b * 4 + i], sibling).start()
            return carry

        lax.fori_loop(0, ROWS // 64, norm, 0)

    def norm_here(b, row):
        def step(i, carry):
            swap = nall.at[rows(row + i * 64, 64)], nall.at[rows(row + ROWS + i * 64, 64)]
            remote(*swap, ps.at[b * 4 + i], pr.at[b * 4 + i], sibling).wait()
            return carry

        lax.fori_loop(0, ROWS // 64, step, 0)

    front(0, 0, 0)
    settle(all_stage)
    stage_sib = rcopy(stage, winv.at[rows(fo * DSH, DSH)], sibling)
    stage_sib.start()
    settle(all_out)
    local[2].wait()
    hidden_grads(0)

    def group(p):
        span = pl.ds(p * 2 * ROWS, 2 * ROWS)

        def tile(n, with_hidden):
            w = lane(n * 256, 256)
            pre = jnp.dot(nall[span, :], winv[:, w], preferred_element_type=F32)
            sig = jax.nn.sigmoid(pre)
            if with_hidden:
                hturn[rows(n * 256, 256), span] = (pre * sig).astype(BF16).T
            mask = jnp.concatenate([maskv[2 * p], maskv[2 * p + 1]], axis=0)[:, :1]
            pgrad[span, w] = (mask * hgr[span, w] * (sig * (1.0 + pre * (1.0 - sig)))).astype(BF16)

        def both(n, carry):
            tile(n, True)
            tile(n + 3, False)
            return carry

        lax.fori_loop(0, HALF // 512, both, 0)

    def turn_normed(p):
        span = pl.ds(p * 2 * ROWS, 2 * ROWS)
        for i, which in enumerate((fs, f)):
            nturn[pl.ds(i * DSH, DSH), span] = nall[span, lane(which * DSH, DSH)].T

    def given(n):
        w = lane(n * 256, 256)
        return remote(part.at[:, w], got.at[:, w], ps.at[8 + n], pr.at[8 + n], sibling)

    def back(g, ref):
        def tile(n, carry):
            w = lane(n * 256, 256)
            ref[:, w] = nt(pgrad[pl.ds(g * ROWS, ROWS), :], winv[w, :])
            if g == 1:
                given(n).start()
            return carry

        lax.fori_loop(0, D // 256, tile, 0)

    here[0].wait()
    fill_mask(1)
    norm_here(0, 0)
    turn_normed(0)
    settle(all_in_w)
    local[3].wait()
    local[4].wait()
    for i, half in ((2, lo), (3, hi)):
        on_chip[i].wait_send()
        on_chip[i].wait_got(winv.at[rows(fs * DSH, DSH), half])
    stage_sib.wait_send()
    stage_sib.wait_got(winv.at[rows(fso * DSH, DSH)])
    group(0)
    back(1, part)
    back(0, ngrad)

    def take(n, carry):
        given(n).wait()
        return carry

    lax.fori_loop(0, D // 256, take, 0)

    def norm_back(i, carry):
        span = rows(i * 64, 64)
        mask = maskv[0, span, :][:, :1]
        pre = conv[span, :]
        sig = jax.nn.sigmoid(pre)
        mixed = feat[0, span, :].astype(F32) + mask * (pre * sig)
        mean = jnp.mean(mixed, axis=-1, keepdims=True)
        centred = mixed - mean
        scale = lax.rsqrt(jnp.mean(centred * centred, axis=-1, keepdims=True) + EPSILON)
        hat = centred * scale
        dn = (ngrad[span, :] + got[span, :]) * gain[...][None, :]
        m1 = jnp.mean(dn, axis=-1, keepdims=True)
        m2 = jnp.mean(dn * hat, axis=-1, keepdims=True)
        total = mask * masked[span, :].astype(F32) + scale * (dn - m1 - hat * m2)
        mix[span, :] = mask * total * (sig * (1.0 + pre * (1.0 - sig)))
        return carry

    lax.fori_loop(0, ROWS // 64, norm_back, 0)

    def tap_chunk(l, carry):
        w = lane(l * LANES, LANES)
        fch[...] = feat[0, :, w].astype(F32)
        for k in range(K):
            t0, t1 = max(0, 15 - k), min(BR, 31 - k)
            size = (t1 - t0) * NB
            term = mix[pl.ds(t0 * NB, size), w] * fch[pl.ds((t0 + k - 15) * NB, size), :]
            sums[pl.ds(k, 1), :] = jnp.sum(term, axis=0, keepdims=True)
        sums[pl.ds(K, 1), :] = jnp.zeros((1, LANES), F32)
        tapp[pl.ds(pl.multiple_of(l * (K + 1), 8), K + 1), :] = sums[...]
        return carry

    lax.fori_loop(0, D // LANES, tap_chunk, 0)

    def spread(make):
        def step(k, carry):
            make(k).start()
            return carry

        lax.fori_loop(1, 16, step, 0)

    def rows24(i):
        return pl.ds(pl.multiple_of(i * 24, 8), 24)

    def one(k):
        to = lax.rem(near + k, 16)
        return remote(tapp.at[rows24(to)], r1.at[k], gs.at[0], gr.at[0], near_dev(to))

    def two(k):
        to = lax.rem(far + k, 16)
        return remote(s1, r2.at[k], gs.at[1], gr.at[1], far_dev(to))

    def three(k):
        to = lax.rem(near + k, 16)
        return remote(s2, r3.at[k], gs.at[2], gr.at[2], near_dev(to))

    def all_here(ref, stage_no):
        every = ref.at[pl.ds(1, 15)]
        remote(every, every, gs.at[stage_no], gr.at[stage_no], sibling).wait()

    def ordered(ref, mine_at):
        def step(i, total):
            return total + ref[lax.rem(mine_at - i + 16, 16)]

        return lax.fori_loop(0, 16, step, jnp.zeros((24, LANES), F32))

    spread(one)
    here[1].wait()
    here[3].wait()
    front(1, 2, 2 * ROWS)
    here[2].wait()
    fill_mask(3)
    r1[0] = tapp[rows24(near), :]
    all_here(r1, 0)
    s1[...] = ordered(r1, near)
    spread(two)
    cot_other.wait()
    cot_sib = rcopy(cots.at[2], cots.at[3], sibling)
    cot_sib.start()
    masked[pl.ds(2 * ROWS, ROWS), :] = turned(2)
    cot_sib.wait()
    masked[pl.ds(3 * ROWS, ROWS), :] = turned(3)
    hidden_grads(1)
    r2[0] = s1[...]
    all_here(r2, 1)
    s2[...] = ordered(r2, far)
    spread(three)
    for g in range(4):
        if g == 2:
            norm_here(1, 2 * ROWS)
            turn_normed(1)
            group(1)
        span = pl.ds(g * ROWS, ROWS)
        masked[span, :] = jnp.where(maskv[g][:, :1] > 0, masked[span, :].astype(F32), 0.0).astype(BF16)

    def gin_tile(i, n):
        return jnp.dot(
            nturn[pl.ds(i * DSH, DSH), :], pgrad[:, lane(n * 256, 256)], preferred_element_type=F32
        ).astype(BF16)

    def give_tile(n, carry):
        stage[:, lane(n * 256, 256)] = gin_tile(0, n)
        return carry

    lax.fori_loop(0, 6, give_tile, 0)
    swaps = [rcopy(stage.at[:, half], ginv.at[:, cols(g)], sibling) for half, g in ((lo, f), (hi, fo))]
    for swap in swaps:
        swap.start()

    def leave(ref, out, w, i):
        return pltpu.make_async_copy(ref.at[:, w], out.at[:, w], os_.at[i])

    def keep_tile(n, carry):
        first, second = lane(f * FSH + n * 256, 256), lane(fo * FSH + n * 256, 256)
        ginv[:, first] = gin_tile(1, n)
        leave(ginv, gin, first, n).start()
        ginv[:, second] = gin_tile(1, n + 3)
        leave(ginv, gin, second, 3 + n).start()
        return carry

    lax.fori_loop(0, 3, keep_tile, 0)

    def gout_tile(n, carry):
        w = lane(n * 256, 256)
        goutv[:, w] = (0.5 * jnp.dot(hturn[...], masked[:, w], preferred_element_type=F32)).astype(BF16)
        leave(goutv, gout, w, 6 + n).start()
        return carry

    lax.fori_loop(0, D // 256, gout_tile, 0)
    for i, (swap, g) in enumerate(zip(swaps, (fs, fso))):
        swap.wait_send()
        swap.wait_got(ginv.at[:, cols(g)])
        leave(ginv, gin, cols(g), 12 + i).start()
    r3[0] = s2[...]
    all_here(r3, 2)

    def lay(k, carry):
        tapp[rows24(lax.rem(near - k + 16, 16)), :] = r3[k] * (1.0 / ROWS)
        return carry

    lax.fori_loop(0, 16, lay, 0)
    for l in range(D // LANES):
        ktot[:, pl.ds(l * LANES, LANES)] = tapp[pl.ds(l * (K + 1), K), :]

    def gone(n, carry):
        leave(ginv, gin, lane(f * FSH + n * 256, 256), n).wait()
        leave(ginv, gin, lane(fo * FSH + n * 256, 256), 3 + n).wait()
        leave(goutv, gout, lane(n * 256, 256), 6 + n).wait()
        leave(goutv, gout, lane((n + 3) * 256, 256), 9 + n).wait()
        return carry

    lax.fori_loop(0, 3, gone, 0)
    for i, g in enumerate((fs, fso)):
        leave(ginv, gin, cols(g), 12 + i).wait()


def on_device(
    frames, occupied_slot_counts, block_frame_rows, order, cotangent, sub_weight, depth_kernel, norm_gain, w_in, w_out
):
    vm, dma = pltpu.VMEM, pltpu.SemaphoreType.DMA
    stages, one = vm((16, 24, LANES), F32), vm((24, LANES), F32)
    gin, gout, total = pl.pallas_call(
        kernel,
        out_shape=[
            jax.ShapeDtypeStruct((DSH, FF), BF16),
            jax.ShapeDtypeStruct((FSH, D), BF16),
            jax.ShapeDtypeStruct((K, D), F32),
        ],
        in_specs=[SM, VM, VM, ANY, VM, VM, ANY, ANY, ANY, ANY],
        out_specs=[ANY, ANY, VM],
        scratch_shapes=[
            vm((NH, 64, LANES), BF16),
            vm((DSH, FF), BF16),
            vm((FSH, D), BF16),
            vm((1, 1, LANES), jnp.int32),
            vm((NDP, LANES), jnp.int32),
            pltpu.SMEM((NDP, LANES), jnp.int32),
            pltpu.SMEM((NB,), jnp.int32),
            vm((NDP, 1, LANES), jnp.int32),
            pltpu.SMEM((NDP, 1, LANES), jnp.int32),
            pltpu.SMEM((NDP,), jnp.int32),
            vm((NDP, 64, LANES), BF16),
            vm((NDP, 64, LANES), BF16),
            vm((2 * NB, 64, LANES), BF16),
            vm((4, NB, LANES), jnp.int32),
            vm((4, ROWS, D), BF16),
            vm((4 * ROWS, D), BF16),
            vm((D, HALF), BF16),
            vm((HALF, D), BF16),
            vm((4 * SSH, D), BF16),
            vm((DSH, HALF), BF16),
            vm((4 * ROWS, HALF), F32),
            vm((4 * ROWS, D), BF16),
            vm((4 * ROWS, HALF), BF16),
            vm((FSH, 4 * ROWS), BF16),
            vm((2 * DSH, 4 * ROWS), BF16),
            vm((4, ROWS, 4 * ROWS), BF16),
            vm((ROWS, 4 * LANES), BF16),
            vm((4, ROWS, LANES), F32),
            vm((K * NB, LANES), F32),
            vm((ROWS, LANES), F32),
            vm((2, ROWS, D), BF16),
            vm((ROWS, D), F32),
            vm((ROWS, D), F32),
            vm((ROWS, D), F32),
            vm((ROWS, D), F32),
            vm((ROWS, D), F32),
            vm((D // LANES * (K + 1), LANES), F32),
            vm((K + 1, LANES), F32),
            stages, one, stages, one, stages,
            dma, dma, dma, dma,
            dma((56,)), dma((56,)), dma((8,)), dma((3,)), dma((3,)), dma((14,)), dma((14,)), dma((14,)),
        ],
        compiler_params=pltpu.CompilerParams(collective_id=1, has_side_effects=True, vmem_limit_bytes=VLIM),
        name="window",
    )(
        occupied_slot_counts, block_frame_rows[0], order, frames[0, 0], depth_kernel, norm_gain,
        cotangent[0, 0].reshape(ROWS, D), w_in, w_out, sub_weight,
    )
    return gin[None], gout[None], total


def solution(mesh):
    placed = (
        P("dp", "fsdp", None, None, None),
        P("fsdp", "dp"),
        P("dp", "fsdp", None),
        P("fsdp", None),
        P("dp", "fsdp", None, None, None),
        P("fsdp", None),
        P(),
        P(),
        P("fsdp", None),
        P("fsdp", None),
    )
    return jax.shard_map(
        on_device,
        mesh=mesh,
        in_specs=placed,
        out_specs=(P("dp", "fsdp", None), P("dp", "fsdp", None), P()),
        check_vma=False,
    )
```
